256 devices in a mesh: rep: 4 (over x), gx: 16 (over y, z_hi, core), gy: 4 (over z_lo).
Axes of the slice: x: 4, y: 4, z: 8 (z_hi: 2, z_lo: 4; z = z_hi * 4 + z_lo), core: 2. Of those that a mesh axis runs over, the one named last changes fastest.
Arguments:
- field: float32 [4, 4, 64, 64, 512], P('rep', None, None, 'gx', 'gy'), may hold values from -4 to 4
- momenta: float32 [4, 4, 64, 64, 512], P('rep', None, None, 'gx', 'gy'), may hold values from -9 to 9
- kappa: float32 [4], P('rep'), may hold values from 0.08 to 0.3
- quartic: float32 [4], P('rep'), may hold values from 0.2 to 1
- acceptance: int32 [4], replicated, may hold values from 0 to 3, as said below
Outputs:
- new_field: float32 [4, 4, 64, 64, 512], P('rep', None, None, 'gx', 'gy')
- new_momenta: float32 [4, 4, 64, 64, 512], P('rep', None, None, 'gx', 'gy')
- energy: float32 [4, 2], P('rep')
The draws below stay inside these ranges and needn't reach their ends.
Inputs may be any that keep to these rules, and one draw needn't show every extreme that they name: acceptance[r] is r - 1, r or r + 1; it pairs replicas (acceptance[acceptance[r]] = r), and all swapped pairs start at the same parity.
All inputs are finite; a program needn't handle non-finite values.
Results may differ from the reference program's by a relative error of at most 0.00016.
Values sent between devices are 32-bit elements; how exact they have to be, the bound alone decides.
No kernel may reach another device: no remote copies, remote signals or barrier semaphores. Data moves between devices by JAX's collectives and lax.ppermute only.
A program may use at most 64 MiB of HBM per device.

```python
import math
import jax
import jax.numpy as jnp

REPS = 4
COMPS = 4
LEAPS = 4
NZ = 64
NX = 64
NY = 512


def draw_momenta(key, part):
    key = jax.random.fold_in(key, 11)
    key_base, key_factor = jax.random.split(key)
    shape = (REPS, COMPS, NZ, NX, NY)
    xpos = jnp.arange(NX, dtype=jnp.float32) / (NX - 1)
    base = jax.random.truncated_normal(key_base, -4.0, 4.0, shape, jnp.float32)
    ramp = 0.6 + 1.2 * xpos
    factor = jnp.exp(jax.random.uniform(key_factor, shape, jnp.float32, jnp.log(0.7), jnp.log(1.4)))
    values = base * factor * ramp[None, None, None, :, None]
    return jnp.clip(values, -9.0, 9.0).astype(jnp.float32)


def draw_acceptance(key, part):
    key = jax.random.fold_in(key, 23)
    key_parity, key_bits = jax.random.split(key)
    selector = jax.random.randint(key_parity, (), 0, 5)
    parity = (selector == 4).astype(jnp.int32)
    bits = jax.random.randint(key_bits, (REPS,), 0, 2)
    bits = jnp.where(parity == 1, bits.at[1].set(1), bits)
    ranks = jnp.arange(REPS, dtype=jnp.int32)
    lower = ((ranks - parity) % 2 == 0) & (ranks >= parity) & (ranks + 1 < REPS) & (bits == 1)
    upper = jnp.roll(lower, 1)
    return (ranks + lower.astype(jnp.int32) - upper.astype(jnp.int32)).astype(jnp.int32)


def block_scale(stream_key, dims, pieces, smallest, largest):
    def one(axis_at, parts):
        steps = jax.random.uniform(jax.random.fold_in(jax.random.fold_in(stream_key, 6), axis_at), (parts,), jnp.float32, smallest / len(pieces), largest / len(pieces))
        return jnp.repeat(jnp.exp(steps), dims[axis_at] // parts).reshape((-1,) + (1,) * (len(dims) - axis_at - 1))

    gain = one(*pieces[0])
    for cut in pieces[1:]:
        gain = gain * one(*cut)
    return gain


def normal_values(key, dims, width, limit, cuts=(), kind=jnp.bfloat16):
    drawn = jax.random.normal(key, dims, jnp.float32) * width
    if len(cuts) > 0:
        drawn = block_scale(key, dims, cuts, -0.22, 0.18) * drawn
    return jnp.clip(drawn, min=-limit, max=limit).astype(kind)


def setup_inputs(seed: int = 0) -> dict:
    arg_keys = jax.random.split(jax.random.key(seed), 6)
    field = normal_values(arg_keys[0], (REPS, COMPS, NZ, NX, NY), 1.0, 4.0, ((0, 4), (3, 16), (4, 4)), jnp.float32)
    momenta = draw_momenta(jax.random.fold_in(arg_keys[5], 71), 0)
    kappa = jnp.clip(jnp.exp(math.log(0.3) - 1.3217559 * jax.random.uniform(arg_keys[2], (REPS,), jnp.float32) ** block_scale(arg_keys[2], (REPS,), ((0, 4),), -0.2, 0.2)), 0.08, 0.3)
    quartic = jnp.clip(jnp.exp(math.log(1.0) - 1.609438 * jax.random.uniform(arg_keys[3], (REPS,), jnp.float32) ** block_scale(arg_keys[3], (REPS,), ((0, 4),), -0.2, 0.2)), 0.2, 1.0)
    acceptance = draw_acceptance(jax.random.fold_in(arg_keys[5], 71), 0)
    return {"field": field, "momenta": momenta, "kappa": kappa, "quartic": quartic, "acceptance": acceptance}


step_size = 0.05


def force_action(phi, kap, qua):
    square = jnp.sum(phi * phi, axis=0)
    nsum = jnp.zeros_like(phi)
    forward = jnp.zeros_like(phi)
    for axis_id in (1, 2, 3):
        upper = jnp.roll(phi, -1, axis=axis_id)
        lower = jnp.roll(phi, 1, axis=axis_id)
        nsum = nsum + upper + lower
        forward = forward + upper
    force = 2.0 * kap * nsum - 2.0 * phi - 4.0 * qua * (square - 1.0) * phi
    density = -2.0 * kap * jnp.sum(phi * forward, axis=0) + square + qua * (square - 1.0) ** 2
    return force, jnp.sum(density)


def trajectory(phi, mom, kap, qua):
    volume = phi.shape[1] * phi.shape[2] * phi.shape[3]
    force, action = force_action(phi, kap, qua)
    start = (0.5 * jnp.sum(mom * mom) + action) / volume
    mom = mom + 0.5 * step_size * force
    for leap in range(LEAPS):
        phi = phi + step_size * mom
        force, action = force_action(phi, kap, qua)
        if leap + 1 < LEAPS:
            mom = mom + step_size * force
        else:
            mom = mom + 0.5 * step_size * force
    finish = (0.5 * jnp.sum(mom * mom) + action) / volume
    return phi, mom, jnp.stack([start, finish])


def reference(field, momenta, kappa, quartic, acceptance):
    fields = []
    moms = []
    energies = []
    for rep_id in range(REPS):
        phi, mom, energy_pair = trajectory(field[rep_id], momenta[rep_id], kappa[rep_id], quartic[rep_id])
        fields.append(phi)
        moms.append(mom)
        energies.append(energy_pair)
    all_fields = jnp.stack(fields)
    all_moms = jnp.stack(moms)
    new_field = jnp.take(all_fields, acceptance, axis=0)
    new_momenta = jnp.take(all_moms, acceptance, axis=0)
    return new_field, new_momenta, jnp.stack(energies)
```

```python
import functools

import jax
import jax.numpy as jnp
from jax import lax
from jax.experimental import pallas as pl
from jax.experimental.pallas import tpu as pltpu
from jax.sharding import PartitionSpec as P

LEAPS = 4
STEP = 0.05
COMPS = 4
NZ = 64
OCT = NZ // 8
WIDE = 4
LANES = 128


def f32(*shape):
    return jax.ShapeDtypeStruct(shape, jnp.float32)


def lanes():
    return lax.broadcasted_iota(jnp.int32, (8, LANES), 1)


def rows():
    return lax.broadcasted_iota(jnp.int32, (8, LANES), 0)


def packed(load):
    octet = lanes() // 16
    out = None
    for o in range(OCT):
        moved = pltpu.roll(load(o), (16 * o + 8) % LANES, 1)
        out = moved if out is None else jnp.where(octet == o, moved, out)
    return out


def split_layer(main, edge, u):
    return (lambda c, o: main[u, c, 8 * o : 8 * o + 8, :], None if edge is None else (lambda c: edge[u, c]))


def joint_layer(ref):
    return (lambda c, o: ref[c, 8 * o : 8 * o + 8, :], lambda c: ref[c, NZ : NZ + 8, :])


def main_eval(down, here, up, mom, put, kap, qua, dt, energy):
    lane, row = (lanes(), rows())
    zero_lane, last_lane = (lane == 0, lane == LANES - 1)
    first_row, last_row = (row == 0, row == 7)
    nsums = {}
    for c in range(COMPS):
        cells = [here[0](c, o) for o in range(OCT)]
        edge = here[1](c)
        ghosts = [pltpu.roll(edge, (120 - 16 * o) % LANES, 1) for o in range(OCT)]
        above = [pltpu.roll(q, 7, 0) for q in cells]
        below = [pltpu.roll(q, 1, 0) for q in cells]
        left = [pltpu.roll(jnp.where(last_lane, g, q), 1, 1) for g, q in zip(ghosts, cells)]
        right = [pltpu.roll(jnp.where(zero_lane, g, q), LANES - 1, 1) for g, q in zip(ghosts, cells)]
        for o in range(OCT):
            z_up = jnp.where(last_row, above[(o + 1) % OCT], above[o])
            z_down = jnp.where(first_row, below[o - 1], below[o])
            nsums[c, o] = (down[0](c, o) + up[0](c, o)) + (left[o] + right[o]) + (z_up + z_down)
    for o in range(OCT):
        cells = [here[0](c, o) for c in range(COMPS)]
        moms = [mom[0](c, o) for c in range(COMPS)]
        square = cells[0] * cells[0]
        for c in range(1, COMPS):
            square = square + cells[c] * cells[c]
        coef = (2.0 - 4.0 * qua) + (4.0 * qua) * square
        dots = None
        results = []
        for c in range(COMPS):
            q, p, nsum = (cells[c], moms[c], nsums[c, o])
            new = p + dt * ((2.0 * kap) * nsum - coef * q)
            results.append((new, q + STEP * new))
            if energy is not None:
                dots = q * nsum if dots is None else dots + q * nsum
                kin = new if energy[1] else p
                energy[0] = energy[0] + 0.5 * (kin * kin)
        if energy is not None:
            energy[0] = energy[0] + (square - kap * dots + qua * ((square - 1.0) * (square - 1.0)))
        for c in range(COMPS):
            put(c, o, *results[c])


def edge_eval(down, here, up, mom, put, kap, qua, dt):
    lane, row = (lanes(), rows())
    slot = lane % 16
    first_row, last_row = (row == 0, row == 7)
    cells = [here[1](c) for c in range(COMPS)]
    square = cells[0] * cells[0]
    for c in range(1, COMPS):
        square = square + cells[c] * cells[c]
    coef = (2.0 - 4.0 * qua) + (4.0 * qua) * square
    results = []
    for c in range(COMPS):
        q = cells[c]
        own = packed(lambda o: here[0](c, o))
        right = pltpu.roll(jnp.where(slot == 8, own, q), LANES - 1, 1)
        left = pltpu.roll(jnp.where(slot == 7, own, q), 1, 1)
        above = pltpu.roll(q, 7, 0)
        below = pltpu.roll(q, 1, 0)
        z_up = jnp.where(last_row, pltpu.roll(above, LANES - 16, 1), above)
        z_down = jnp.where(first_row, pltpu.roll(below, 16, 1), below)
        nsum = (down[1](c) + up[1](c)) + (left + right) + (z_up + z_down)
        new = mom[1](c) + dt * ((2.0 * kap) * nsum - coef * q)
        results.append((new, q + STEP * new))
    for c in range(COMPS):
        put(c, *results[c])


def ingest_kernel(flags, field, momenta, q, p, edges, far, farther, near):
    for core in range(2):

        @pl.when(flags[0] == core)
        def _():
            for u in range(WIDE):
                x = u if core == 0 else WIDE - 1 - u
                for c in range(COMPS):
                    for k, (src, dst) in enumerate(((field, q), (momenta, p))):
                        value = src[c, pl.ds(x, NZ, stride=WIDE), :]
                        dst[u, c] = value
                        edges[k, u, c] = packed(lambda o: value[8 * o : 8 * o + 8, :])
                        if k == 0 and u == 0:
                            far[c] = value
                        if k == 0 and u == 1:
                            farther[0, c] = value
                        if k == 1 and u == 0:
                            farther[1, c] = value
                        if k == 0 and u == WIDE - 1:
                            near[c] = value


def ghost_kernel(flags, first, second, qg, pg, near, far):
    left_slots = lanes() % 16 < 8
    odd = jnp.broadcast_to(flags[1], (8, LANES)) == 1
    take_first = left_slots == odd
    for k, dst in enumerate((qg, pg)):
        for u in range(WIDE):
            for c in range(COMPS):
                value = jnp.where(take_first, first[k, u, c], second[k, u, c])
                dst[u, c] = value
                if k == 0 and u == WIDE - 1:
                    near[c] = value
                if k == 0 and u == 0:
                    far[0, c] = value
                if k == 0 and u == 1:
                    far[1, c] = value
                if k == 1 and u == 0:
                    far[2, c] = value


def putters(q, p, qg, pg, u, extra):
    def put(c, o, new_p, new_q):
        p[u, c, 8 * o : 8 * o + 8, :] = new_p
        q[u, c, 8 * o : 8 * o + 8, :] = new_q
        for ref in extra:
            ref[c, 8 * o : 8 * o + 8, :] = new_q

    def put_edge(c, new_p, new_q):
        pg[u, c] = new_p
        qg[u, c] = new_q
        for ref in extra:
            ref[c, NZ : NZ + 8, :] = new_q

    return put, put_edge


def first_kernel(par, qm, qg, pm, pg, far, near, near_g, q, g, p, h, msg, msg_near, energy):
    kap, qua = (par[0], par[1])
    layers = [split_layer(qm, qg, u) for u in range(WIDE)]
    moms = [split_layer(pm, pg, u) for u in range(WIDE)]
    low = (lambda c, o: far[c, 8 * o : 8 * o + 8, :], None)
    high = (lambda c, o: near[c, 8 * o : 8 * o + 8, :], lambda c: near_g[c])
    around = [low, *layers, high]
    total = [jnp.zeros((8, LANES), jnp.float32), False]
    for u in (1, 3, 0, 2):
        extra = [msg] if u == 1 else [msg_near] if u == WIDE - 1 else []
        put, put_edge = putters(q, p, g, h, u, extra)
        main_eval(around[u], around[u + 1], around[u + 2], moms[u], put, kap, qua, 0.5 * STEP, total)
        if u > 0:
            edge_eval(around[u], around[u + 1], around[u + 2], moms[u], put_edge, kap, qua, 0.5 * STEP)
    energy[...] = total[0]


def second_kernel(
    par, qm, qg, pm, pg, near, far0, far0g, beyond, own0, own0g, own0pg,
    q, g, p, h, hq, hp, zero, msg, msg_near, fixed, fixed_p,
):
    kap, qua = (par[0], par[1])
    outer = (lambda c, o: beyond[0, c, 8 * o : 8 * o + 8, :], lambda c: far0g[1, c])
    halo = (lambda c, o: far0[c, 8 * o : 8 * o + 8, :], lambda c: far0g[0, c])
    inner = (lambda c, o: own0[c, 8 * o : 8 * o + 8, :], lambda c: own0g[0, c])
    inside = (None, lambda c: own0g[1, c])
    halo_mom = (lambda c, o: beyond[1, c, 8 * o : 8 * o + 8, :], lambda c: far0g[2, c])
    halo_step(outer, halo, inner, halo_mom, hq, hp, kap, qua, 0.5 * STEP)

    def put_zero(c, new_p, new_q):
        fixed[c] = new_q
        fixed_p[c] = new_p

    edge_eval(halo, inner, inside, (None, lambda c: own0pg[0, c]), put_zero, kap, qua, 0.5 * STEP)
    layers = [split_layer(qm, qg, u) for u in range(WIDE)]
    moms = [split_layer(pm, pg, u) for u in range(WIDE)]
    layers[0] = (layers[0][0], lambda c: fixed[c])
    moms[0] = (moms[0][0], lambda c: fixed_p[c])
    own_step(layers, moms, joint_layer(hq), joint_layer(near), q, g, p, h, zero, msg, msg_near, kap, qua)


def halo_step(outer, halo, inner, mom, hq, hp, kap, qua, dt):
    def put(c, o, new_p, new_q):
        hp[c, 8 * o : 8 * o + 8, :] = new_p
        hq[c, 8 * o : 8 * o + 8, :] = new_q

    def put_edge(c, new_p, new_q):
        hp[c, NZ : NZ + 8, :] = new_p
        hq[c, NZ : NZ + 8, :] = new_q

    main_eval(outer, halo, inner, mom, put, kap, qua, dt, None)
    edge_eval(outer, halo, inner, mom, put_edge, kap, qua, dt)


def own_step(layers, moms, low, high, q, g, p, h, zero, msg, msg_near, kap, qua):
    around = [low, *layers, high]
    if zero is not None:
        for c in range(COMPS):
            for o in range(OCT):
                zero[c, 8 * o : 8 * o + 8, :] = layers[0][0](c, o)
            zero[c, NZ : NZ + 8, :] = layers[0][1](c)
    for u in (1, 3, 0, 2):
        extra = []
        if u == 1 and msg is not None:
            extra = [msg]
        if u == WIDE - 1:
            extra = [msg_near]
        put, put_edge = putters(q, p, g, h, u, extra)
        main_eval(around[u], around[u + 1], around[u + 2], moms[u], put, kap, qua, STEP, None)
        edge_eval(around[u], around[u + 1], around[u + 2], moms[u], put_edge, kap, qua, STEP)


def middle_kernel(last, par, qm, qg, pm, pg, near, beyond, hq0, hp0, zero0, *outs):
    kap, qua = (par[0], par[1])
    if last:
        q, g, p, h, hq, hp, zero, msg_near = outs
        msg = None
    else:
        q, g, p, h, hq, hp, zero, msg, msg_near = outs
    halo_step(joint_layer(beyond), joint_layer(hq0), joint_layer(zero0), joint_layer(hp0), hq, hp, kap, qua, STEP)
    layers = [split_layer(qm, qg, u) for u in range(WIDE)]
    moms = [split_layer(pm, pg, u) for u in range(WIDE)]
    own_step(layers, moms, joint_layer(hq), joint_layer(near), q, g, p, h, zero, msg, msg_near, kap, qua)


def final_kernel(par, qm, qg, pm, near, beyond, hq0, hp0, zero0, start, p, energy, hq):
    kap, qua = (par[0], par[1])
    halo = joint_layer(hq0)

    def put_halo(c, o, new_p, new_q):
        hq[c, 8 * o : 8 * o + 8, :] = new_q

    main_eval(joint_layer(beyond), halo, joint_layer(zero0), joint_layer(hp0), put_halo, kap, qua, STEP, None)
    around = [joint_layer(hq), *[split_layer(qm, qg, u) for u in range(WIDE)], joint_layer(near)]
    total = [jnp.zeros((8, LANES), jnp.float32), True]
    for u in range(WIDE):

        def put(c, o, new_p, new_q, u=u):
            p[u, c, 8 * o : 8 * o + 8, :] = new_p

        mom = split_layer(pm, None, u)
        main_eval(around[u], around[u + 1], around[u + 2], mom, put, kap, qua, 0.5 * STEP, total)
    before = jnp.sum(start[...], axis=0, keepdims=True)
    after = jnp.sum(total[0], axis=0, keepdims=True)
    row = rows()
    energy[...] = jnp.where(row == 0, before, jnp.where(row == 1, after, 0.0))


def place_kernel(flags, own, below, above, out):
    for core in range(2):
        for pick, src in ((0, own), (1, below), (2, above)):

            @pl.when((flags[0] == core) & (flags[2] == pick))
            def _():
                for u in range(WIDE):
                    x = u if core == 0 else WIDE - 1 - u
                    for c in range(COMPS):
                        out[c, pl.ds(x, NZ, stride=WIDE), :] = src[u, c]


def run(kernel, outs, scalars, arrays, scratch=(), cost=400_000):
    vmem = pl.BlockSpec(memory_space=pltpu.VMEM)
    smem = pl.BlockSpec(memory_space=pltpu.SMEM)
    return pl.pallas_call(
        kernel,
        out_shape=outs,
        in_specs=[smem] * len(scalars) + [vmem] * len(arrays),
        out_specs=[vmem] * len(outs),
        scratch_shapes=list(scratch),
        cost_estimate=pl.CostEstimate(flops=cost * 4, bytes_accessed=cost, transcendentals=0),
    )(*scalars, *arrays)


def pair_swap(value, axis, other):
    return lax.ppermute(value, axis, [(i, other(i)) for i in range(lax.axis_size(axis))])


def local(field, momenta, kappa, quartic, acceptance):
    gx, gy = (lax.axis_size("gx"), lax.axis_size("gy"))
    volume = NZ * WIDE * LANES * gx * gy
    position = lax.axis_index("rep")
    partner = acceptance[position]
    pick = jnp.where(partner == position - 1, 1, jnp.where(partner == position + 1, 2, 0))
    flags = jnp.stack([lax.axis_index("gx") % 2, lax.axis_index("gy") % 2, pick]).astype(jnp.int32)
    par = jnp.concatenate([kappa, quartic])

    def far(value):
        return pair_swap(value, "gx", lambda i: (i + 1) % gx if i % 2 == 1 else (i - 1) % gx)

    def near(value):
        return pair_swap(value, "gx", lambda i: i ^ 1)

    def beside(value, parity):
        return pair_swap(value, "gy", lambda i: (i + 1) % gy if i % 2 == parity else (i - 1) % gy)

    state = [f32(WIDE, COMPS, NZ, LANES), f32(WIDE, COMPS, 8, LANES)] * 2
    layer, edge = (f32(COMPS, NZ, LANES), f32(COMPS, 8, LANES))
    joint = f32(COMPS, NZ + 8, LANES)
    pair = f32(2, COMPS, NZ, LANES)

    qm, pm, edges, far0, farther, near0 = run(
        ingest_kernel,
        [state[0], state[0], f32(2, WIDE, COMPS, 8, LANES), layer, pair, layer],
        [flags],
        [field.reshape(COMPS, NZ * WIDE, LANES), momenta.reshape(COMPS, NZ * WIDE, LANES)],
    )
    far_main = far(far0)
    near_main = near(near0)
    first, second = (beside(edges, 0), beside(edges, 1))
    beyond0 = far(farther)
    qg, pg, near_g, far_g = run(
        ghost_kernel, [state[1], state[1], edge, f32(3, COMPS, 8, LANES)], [flags], [first, second], cost=100_000
    )
    near_ghost = near(near_g)
    q1, g1, p1, h1, msg1, to_near, start = run(
        first_kernel,
        state + [joint, joint, f32(8, LANES)],
        [par],
        [qm, qg, pm, pg, far_main, near_main, near_ghost],
    )
    beyond1 = far(msg1)
    near1 = near(to_near)
    far_ghost = far(far_g)
    q2, g2, p2, h2, hq, hp, zero, msg2, to_near = run(
        second_kernel,
        state + [joint] * 5,
        [par],
        [q1, g1, p1, h1, near1, far_main, far_ghost, beyond0, far0, qg, pg],
        scratch=[pltpu.VMEM((COMPS, 8, LANES), jnp.float32)] * 2,
    )
    beyond2 = far(msg2)
    near2 = near(to_near)
    q3, g3, p3, h3, hq, hp, zero, msg3, to_near = run(
        functools.partial(middle_kernel, False),
        state + [joint] * 5,
        [par],
        [q2, g2, p2, h2, near2, beyond1, hq, hp, zero],
    )
    beyond3 = far(msg3)
    near3 = near(to_near)
    q4, g4, p4, h4, hq, hp, zero, to_near = run(
        functools.partial(middle_kernel, True),
        state + [joint] * 4,
        [par],
        [q3, g3, p3, h3, near3, beyond2, hq, hp, zero],
    )
    near4 = near(to_near)
    up = [(i, i + 1) for i in range(lax.axis_size("rep") - 1)]
    down = [(i + 1, i) for i in range(lax.axis_size("rep") - 1)]
    below_q, above_q = (lax.ppermute(q4, "rep", up), lax.ppermute(q4, "rep", down))
    p5, energy = run(
        final_kernel,
        [state[0], f32(8, LANES)],
        [par],
        [q4, g4, p4, near4, beyond3, hq, hp, zero, start],
        scratch=[pltpu.VMEM((COMPS, NZ + 8, LANES), jnp.float32)],
    )
    below_p, above_p = (lax.ppermute(p5, "rep", up), lax.ppermute(p5, "rep", down))

    def summed(value, axis):
        bit = 1
        while bit < lax.axis_size(axis):
            value = value + pair_swap(value, axis, lambda i, bit=bit: i ^ bit)
            bit *= 2
        return value

    energy = summed(summed(energy, "gx"), "gy")
    energy = (jnp.sum(energy[:2], axis=1) / volume)[None, :]
    shape = f32(COMPS, NZ * WIDE, LANES)
    (new_q,) = run(place_kernel, [shape], [flags], [q4, below_q, above_q], cost=200_000)
    (new_p,) = run(place_kernel, [shape], [flags], [p5, below_p, above_p], cost=200_000)
    return (new_q.reshape(field.shape), new_p.reshape(field.shape), energy)


def solution(mesh):
    placed = (
        P("rep", None, None, "gx", "gy"),
        P("rep", None, None, "gx", "gy"),
        P("rep"),
        P("rep"),
        P(),
    )
    return jax.shard_map(
        local,
        mesh=mesh,
        in_specs=placed,
        out_specs=(
            P("rep", None, None, "gx", "gy"),
            P("rep", None, None, "gx", "gy"),
            P("rep", None),
        ),
        check_vma=False,
    )
```

```python
import functools

import jax
import jax.numpy as jnp
from jax import lax
from jax.experimental import pallas as pl
from jax.experimental.pallas import tpu as pltpu
from jax.sharding import PartitionSpec as P

LEAPS = 4
STEP = 0.05
COMPS = 4
NZ = 64
OCT = NZ // 8
WIDE = 4
LANES = 128


def f32(*shape):
    return jax.ShapeDtypeStruct(shape, jnp.float32)


def lanes():
    return lax.broadcasted_iota(jnp.int32, (8, LANES), 1)


def rows():
    return lax.broadcasted_iota(jnp.int32, (8, LANES), 0)


def packed(load):
    octet = lanes() // 16
    out = None
    for o in range(OCT):
        moved = pltpu.roll(load(o), (16 * o + 8) % LANES, 1)
        out = moved if out is None else jnp.where(octet == o, moved, out)
    return out


def layer_of(main, edge=None):
    return (lambda c, o: main[c, 8 * o : 8 * o + 8, :], None if edge is None else (lambda c: edge[c]))


def joint(ref):
    return (lambda c, o: ref[c, 8 * o : 8 * o + 8, :], lambda c: ref[c, NZ : NZ + 8, :])


def store_main(q, p):
    def put(c, o, new_p, new_q):
        if p is not None:
            p[c, 8 * o : 8 * o + 8, :] = new_p
        if q is not None:
            q[c, 8 * o : 8 * o + 8, :] = new_q

    return put


def store_edge(q, p):
    def put(c, new_p, new_q):
        p[c, NZ : NZ + 8, :] = new_p
        q[c, NZ : NZ + 8, :] = new_q

    return put


def main_eval(down, here, up, mom, put, kap, qua, dt, energy):
    lane, row = (lanes(), rows())
    zero_lane, last_lane = (lane == 0, lane == LANES - 1)
    first_row, last_row = (row == 0, row == 7)
    nsums = {}
    for c in range(COMPS):
        cells = [here[0](c, o) for o in range(OCT)]
        edge = here[1](c)
        ghosts = [pltpu.roll(edge, (120 - 16 * o) % LANES, 1) for o in range(OCT)]
        above = [pltpu.roll(q, 7, 0) for q in cells]
        below = [pltpu.roll(q, 1, 0) for q in cells]
        left = [pltpu.roll(jnp.where(last_lane, g, q), 1, 1) for g, q in zip(ghosts, cells)]
        right = [pltpu.roll(jnp.where(zero_lane, g, q), LANES - 1, 1) for g, q in zip(ghosts, cells)]
        for o in range(OCT):
            z_up = jnp.where(last_row, above[(o + 1) % OCT], above[o])
            z_down = jnp.where(first_row, below[o - 1], below[o])
            nsums[c, o] = (down[0](c, o) + up[0](c, o)) + (left[o] + right[o]) + (z_up + z_down)
    waiting = []
    for o in range(OCT):
        cells = [here[0](c, o) for c in range(COMPS)]
        moms = [mom[0](c, o) for c in range(COMPS)]
        square = cells[0] * cells[0]
        for c in range(1, COMPS):
            square = square + cells[c] * cells[c]
        coef = (2.0 - 4.0 * qua) + (4.0 * qua) * square
        dots = None
        results = []
        for c in range(COMPS):
            q, p, nsum = (cells[c], moms[c], nsums[c, o])
            new = p + dt * ((2.0 * kap) * nsum - coef * q)
            results.append((new, q + STEP * new))
            if energy is not None:
                dots = q * nsum if dots is None else dots + q * nsum
                kin = new if energy[1] else p
                energy[0] = energy[0] + 0.5 * (kin * kin)
        if energy is not None:
            energy[0] = energy[0] + (square - kap * dots + qua * ((square - 1.0) * (square - 1.0)))
        waiting.append((o, results))
        while len(waiting) > (2 if o < OCT - 1 else 0):
            at, ready = waiting.pop(0)
            for c in range(COMPS):
                put(c, at, *ready[c])


def edge_eval(jobs, kap, qua, dt):
    lane, row = (lanes(), rows())
    slot = lane % 16
    first_row, last_row = (row == 0, row == 7)
    results = []
    for down, here, up, mom, _ in jobs:
        cells = [here[1](c) for c in range(COMPS)]
        square = cells[0] * cells[0]
        for c in range(1, COMPS):
            square = square + cells[c] * cells[c]
        coef = (2.0 - 4.0 * qua) + (4.0 * qua) * square
        for c in range(COMPS):
            q = cells[c]
            own = packed(lambda o: here[0](c, o))
            right = pltpu.roll(jnp.where(slot == 8, own, q), LANES - 1, 1)
            left = pltpu.roll(jnp.where(slot == 7, own, q), 1, 1)
            above = pltpu.roll(q, 7, 0)
            below = pltpu.roll(q, 1, 0)
            z_up = jnp.where(last_row, pltpu.roll(above, LANES - 16, 1), above)
            z_down = jnp.where(first_row, pltpu.roll(below, 16, 1), below)
            nsum = (down[1](c) + up[1](c)) + (left + right) + (z_up + z_down)
            new = mom[1](c) + dt * ((2.0 * kap) * nsum - coef * q)
            results.append((new, q + STEP * new))
    for job, (*_, put) in enumerate(jobs):
        for c in range(COMPS):
            put(c, *results[job * COMPS + c])


def ingest_kernel(flags, field, momenta, *refs):
    mains, messages, (held, sems) = ((refs[:4], refs[4:8]), refs[8:10], refs[10:])
    copies = {
        (k, c): pltpu.make_async_copy(src.at[c], held.at[k, c], sems.at[k, c])
        for c in range(COMPS)
        for k, src in enumerate((field, momenta))
    }
    for copy in copies.values():
        copy.start()
    low = lanes() % 16 < 8
    odd = jnp.broadcast_to(flags[1], (8, LANES)) == 1
    for c in range(COMPS):
        copies[0, c].wait()
        copies[1, c].wait()
        for core in range(2):

            @pl.when(flags[0] == core)
            def _():
                for u in range(WIDE):
                    x = u if core == 0 else WIDE - 1 - u
                    packs = []
                    for k in range(2):
                        value = held[k, c, pl.ds(x, NZ, stride=WIDE), :]
                        mains[k][u][c] = value
                        packs.append(packed(lambda o: value[8 * o : 8 * o + 8, :]))
                    right = jnp.where(low, packs[0], pltpu.roll(packs[1], 8, 1))
                    left = jnp.where(low, pltpu.roll(packs[0], LANES - 8, 1), packs[1])
                    messages[0][u, c] = jnp.where(odd, left, right)
                    messages[1][u, c] = jnp.where(odd, right, left)


def ghost_kernel(flags, first, second, m1, k0, qg, pg, near, far):
    low = lanes() % 16 < 8
    odd = jnp.broadcast_to(flags[1], (8, LANES)) == 1
    for u in range(WIDE):
        for c in range(COMPS):
            left = jnp.where(odd, first[u, c], second[u, c])
            right = jnp.where(odd, second[u, c], first[u, c])
            q = jnp.where(low, left, pltpu.roll(right, 8, 1))
            p = jnp.where(low, pltpu.roll(left, LANES - 8, 1), right)
            qg[u, c] = q
            pg[u, c] = p
            if u == WIDE - 1:
                near[c] = q
            if u == 0:
                far[c, 2 * NZ + 8 : 2 * NZ + 16, :] = p
                far[c, 2 * NZ + 16 :, :] = q
            if u == 1:
                far[c, NZ : NZ + 8, :] = q
    for c in range(COMPS):
        far[c, :NZ, :] = m1[c]
        far[c, NZ + 8 : 2 * NZ + 8, :] = k0[c]


def fresh():
    return jnp.zeros((8, LANES), jnp.float32)


def step(around, moms, outs, kap, qua, dt, energy=None, edges=True):
    spans = [around[i : i + 3] for i in range(len(moms))]
    if edges:
        jobs = [(*span, mom, store_edge(*out)) for span, mom, out in zip(spans, moms, outs)]
        edge_eval(jobs, kap, qua, dt)
    for span, mom, out in zip(spans, moms, outs):
        main_eval(*span, mom, store_main(*out), kap, qua, dt, energy)


def inner_start(
    par, far, m0, m1, m2, m3, k0, k1, k2, k3, qg, pg, near, near_g, z, zp, q1, p1, q2, p2, q3, p3, energy
):
    kap, qua = (par[0], par[1])
    around = [layer_of(main, qg.at[u]) for u, main in enumerate((m0, m1, m2, m3))] + [layer_of(near, near_g)]
    total = [fresh(), False]
    held = [layer_of(mom, pg.at[u + 1]) for u, mom in enumerate((k1, k2, k3))]
    step(around, held, [(q1, p1), (q2, p2), (q3, p3)], kap, qua, 0.5 * STEP, total)
    store = store_main(z, zp)
    main_eval(layer_of(far), around[0], around[1], layer_of(k0), store, kap, qua, 0.5 * STEP, total)
    energy[...] = total[0]


def part_of(ref, main, edge):
    return (lambda c, o: ref[c, main + 8 * o : main + 8 * o + 8, :], lambda c: ref[c, edge : edge + 8, :])


def second_kernel(par, beyond, m0, qg, pg, z, q1, p1, q2, zg, zpg, n1, r1):
    kap, qua = (par[0], par[1])
    down, up = (part_of(beyond, 0, 2 * NZ + 16), (None, lambda c: qg[1, c]))

    def put(c, new_p, new_q):
        zpg[c] = new_p
        zg[c] = new_q

    edge_eval([(down, layer_of(m0, qg.at[0]), up, (None, lambda c: pg[0, c]), put)], kap, qua, 0.5 * STEP)
    step([layer_of(z, zg), joint(q1), joint(q2)], [joint(p1)], [(n1, r1)], kap, qua, STEP)


def third_kernel(
    par, beyond, far, m0, qg, z, zg, zp, zpg, old1, q1, p1, q2, hq, hp, nz, nzp, n1, r1, msg
):
    kap, qua = (par[0], par[1])
    halo = (layer_of(far)[0], part_of(beyond, 0, 2 * NZ + 16)[1])
    mom = part_of(beyond, NZ + 8, 2 * NZ + 8)
    step([part_of(beyond, 0, NZ), halo, layer_of(m0, qg.at[0])], [mom], [(hq, hp)], kap, qua, 0.5 * STEP)
    step([joint(hq), layer_of(z, zg), joint(old1)], [layer_of(zp, zpg)], [(nz, nzp)], kap, qua, STEP)
    step([joint(nz), joint(q1), joint(q2)], [joint(p1)], [(n1, r1)], kap, qua, STEP)
    for c in range(COMPS):
        msg[c] = n1[c, :NZ, :]


def outer_kernel(par, beyond, hq, hp, zold, zold_g, z, zp, old1, q1, p1, q2, nhq, nhp, nz, nzp, n1, r1):
    kap, qua = (par[0], par[1])
    step([joint(beyond), joint(hq), layer_of(zold, zold_g)], [joint(hp)], [(nhq, nhp)], kap, qua, STEP)
    step([joint(nhq), joint(z), joint(old1)], [joint(zp)], [(nz, nzp)], kap, qua, STEP)
    step([joint(nz), joint(q1), joint(q2)], [joint(p1)], [(n1, r1)], kap, qua, STEP)


def inner_kernel(par, q1, q2, p2, q3, p3, near, n2, r2, n3, r3):
    around = [joint(q1), joint(q2), joint(q3), joint(near)]
    step(around, [joint(p2), joint(p3)], [(n2, r2), (n3, r3)], par[0], par[1], STEP)


def inner_final(par, q1, q2, p2, q3, p3, near, r2, r3, energy):
    around = [joint(q1), joint(q2), joint(q3), joint(near)]
    total = [fresh(), True]
    outs = [(None, r2), (None, r3)]
    step(around, [joint(p2), joint(p3)], outs, par[0], par[1], 0.5 * STEP, total, False)
    energy[...] = total[0]


def outer_last(par, beyond, hq, hp, zold, z, zp, old1, q1, p1, q2, q3, nhq, nhp, nz, nzp, whole, r1, energy):
    kap, qua = (par[0], par[1])
    step([joint(beyond), joint(hq), joint(zold)], [joint(hp)], [(nhq, nhp)], kap, qua, STEP)
    step([joint(nhq), joint(z), joint(old1)], [joint(zp)], [(nz, nzp)], kap, qua, STEP)
    for u, ref in enumerate((nz, q1, q2, q3)):
        for c in range(COMPS):
            whole[u, c] = ref[c, :NZ, :]
    total = [fresh(), True]
    step([joint(nz), joint(q1), joint(q2)], [joint(p1)], [(None, r1)], kap, qua, 0.5 * STEP, total, False)
    energy[...] = total[0]


def final_kernel(par, beyond, hq, hp, zold, z, zp, q1, r1, r2, r3, start, some, more, whole, energy, nhq):
    kap, qua = (par[0], par[1])
    main_eval(layer_of(beyond), joint(hq), joint(zold), joint(hp), store_main(nhq, None), kap, qua, STEP, None)
    total = [some[...] + more[...], True]
    store = store_main(None, whole.at[0])
    main_eval(layer_of(nhq), joint(z), joint(q1), joint(zp), store, kap, qua, 0.5 * STEP, total)
    for u, ref in enumerate((r1, r2, r3)):
        for c in range(COMPS):
            whole[u + 1, c] = ref[c]
    before = jnp.sum(start[...], axis=0, keepdims=True)
    after = jnp.sum(total[0], axis=0, keepdims=True)
    row = rows()
    energy[...] = jnp.where(row == 0, before, jnp.where(row == 1, after, 0.0))


def place_kernel(flags, own, first, second, out):
    for core in range(2):
        for pick, src in enumerate((own, first, second)):

            @pl.when((flags[0] == core) & (flags[1] == pick))
            def _():
                for u in range(WIDE):
                    x = u if core == 0 else WIDE - 1 - u
                    for c in range(COMPS):
                        out[c, pl.ds(x, NZ, stride=WIDE), :] = src[u, c]


def add_kernel(one, two, out):
    out[...] = one[...] + two[...]


def run(kernel, outs, scalars, arrays, scratch=(), cost=1000, held=True, raw=False, after=()):
    vmem = pl.BlockSpec(memory_space=pltpu.VMEM)
    smem = pl.BlockSpec(memory_space=pltpu.SMEM)
    place = pl.BlockSpec(memory_space=pltpu.HBM) if raw else vmem
    if held:
        outs = [pltpu.VMEM(out.shape, out.dtype) for out in outs]
    given = len(scalars) + len(arrays)

    def body(*refs):
        kernel(*refs[:given], *refs[given + len(after) :])

    return pl.pallas_call(
        body,
        out_shape=outs,
        in_specs=[smem] * len(scalars) + [place] * len(arrays) + [pl.BlockSpec(memory_space=pl.ANY)] * len(after),
        out_specs=[vmem] * len(outs),
        scratch_shapes=list(scratch),
        cost_estimate=pl.CostEstimate(flops=cost * 4, bytes_accessed=cost, transcendentals=0),
        compiler_params=pltpu.CompilerParams(vmem_limit_bytes=12 * 1024 * 1024),
    )(*scalars, *arrays, *after)


def pair_swap(value, axis, other):
    return lax.ppermute(value, axis, [(i, other(i)) for i in range(lax.axis_size(axis)) if other(i) is not None])


def local(field, momenta, kappa, quartic, acceptance):
    gx, gy, reps = (lax.axis_size("gx"), lax.axis_size("gy"), lax.axis_size("rep"))
    volume = NZ * WIDE * LANES * gx * gy
    core = lax.axis_index("gx") % 2
    flags = jnp.stack([core, lax.axis_index("gy") % 2]).astype(jnp.int32)
    position = lax.axis_index("rep")
    partner = acceptance[position]
    pick = jnp.where(partner == position, 0, jnp.where(partner == position ^ 1, 1, 2))
    choice = jnp.stack([core, pick]).astype(jnp.int32)
    par = jnp.concatenate([kappa, quartic])

    def far(value):
        return pair_swap(value, "gx", lambda i: (i + 1) % gx if i % 2 == 1 else (i - 1) % gx)

    def near(value):
        return pair_swap(value, "gx", lambda i: i ^ 1)

    def beside(value, parity):
        return pair_swap(value, "gy", lambda i: (i + 1) % gy if i % 2 == parity else (i - 1) % gy)

    def exchanged(value):
        first = pair_swap(value, "rep", lambda i: i ^ 1 if i ^ 1 < reps else None)
        second = pair_swap(value, "rep", lambda i: ((i - 1) ^ 1) + 1 if 0 < i and ((i - 1) ^ 1) + 1 < reps else None)
        return (first, second)

    main, both = (f32(COMPS, NZ, LANES), f32(COMPS, NZ + 8, LANES))
    edges, whole, vreg = (f32(WIDE, COMPS, 8, LANES), f32(WIDE, COMPS, NZ, LANES), f32(8, LANES))
    edge = f32(COMPS, 8, LANES)

    m0, m1, m2, m3, k0, k1, k2, k3, to_first, to_second = run(
        ingest_kernel,
        [main] * 8 + [edges] * 2,
        [flags],
        [
            pltpu.with_memory_space_constraint(value.reshape(COMPS, NZ * WIDE, LANES), pltpu.HBM)
            for value in (field, momenta)
        ],
        scratch=[pltpu.VMEM((2, COMPS, NZ * WIDE, LANES), jnp.float32), pltpu.SemaphoreType.DMA((2, COMPS))],
        raw=True,
    )
    far0, near0 = (far(m0), near(m3))
    first, second = (beside(to_first, 0), beside(to_second, 1))
    qg, pg, near_g, to_far = run(
        ghost_kernel, [edges, edges, edge, f32(COMPS, 2 * NZ + 24, LANES)], [flags], [first, second, m1, k0]
    )
    near_ghost, beyond0 = (near(near_g), far(to_far))
    z1, zp1, a1, b1, a2, b2, a3, b3, start = run(
        inner_start,
        [main, main] + [both] * 6 + [vreg],
        [par],
        [far0, m0, m1, m2, m3, k0, k1, k2, k3, qg, pg, near0, near_ghost],
    )
    beyond1, near1 = (far(a1), near(a3))
    c2, d2, c3, d3 = run(inner_kernel, [both] * 4, [par], [a1, a2, b2, a3, b3, near1], after=[choice])
    zg1, zpg1, c1, d1 = run(
        second_kernel,
        [edge] * 2 + [both] * 2,
        [par],
        [beyond0, m0, qg, pg, z1, a1, b1, a2],
        after=[c2],
    )
    beyond2 = far(c1)
    near2 = near(c3)
    hq1, hp1, z2, zp2, e1, f1, msg = run(
        third_kernel,
        [both] * 6 + [main],
        [par],
        [beyond0, far0, m0, qg, z1, zg1, zp1, zpg1, a1, c1, d1, c2],
    )
    beyond3 = far(msg)
    e2, f2, e3, f3 = run(inner_kernel, [both] * 4, [par], [c1, c2, d2, c3, d3, near2], after=[hq1])
    near3 = near(e3)
    hq2, hp2, z3, zp3, g1, h1 = run(
        outer_kernel,
        [both] * 6,
        [par],
        [beyond1, hq1, hp1, z1, zg1, z2, zp2, c1, e1, f1, e2],
    )
    g2, h2, g3, h3 = run(inner_kernel, [both] * 4, [par], [e1, e2, f2, e3, f3, near3], after=[hq2])
    near4 = near(g3)
    hq3, hp3, z4, zp4, final_q, r1, some = run(
        outer_last,
        [both] * 4 + [whole, main, vreg],
        [par],
        [beyond2, hq2, hp2, z2, z3, zp3, e1, g1, h1, g2, g3],
    )
    r2, r3, more = run(inner_final, [main, main, vreg], [par], [g1, g2, h2, g3, h3, near4], after=[hq3])
    first_q, second_q = exchanged(final_q)
    final_p, energy = run(
        final_kernel,
        [whole, vreg],
        [par],
        [beyond3, hq3, hp3, z3, z4, zp4, g1, r1, r2, r3, start, some, more],
        scratch=[pltpu.VMEM((COMPS, NZ, LANES), jnp.float32)],
    )
    first_p, second_p = exchanged(final_p)

    def placed(own, first, second):
        shape = f32(COMPS, NZ * WIDE, LANES)
        return run(place_kernel, [shape], [choice], [own, first, second], held=False)[0].reshape(field.shape)

    def summed(value, axes, other, after=None):
        sizes = [lax.axis_size(axis) for axis in axes]
        pairs = []
        for i in range(sizes[0]):
            for j in range(sizes[1] if len(axes) > 1 else 1):
                to = other(i, j)
                pairs.append((i, to[0]) if len(axes) == 1 else (i * sizes[1] + j, to[0] * sizes[1] + to[1]))
        got = lax.ppermute(value, axes, pairs)
        if after is None:
            return value + got
        later = pltpu.with_memory_space_constraint(after, pltpu.HBM)
        return run(add_kernel, [vreg], [], [value, got], after=[later])[0]

    new_q = placed(final_q, first_q, second_q)
    new_p = placed(final_p, first_p, second_p)
    energy = energy + near(energy)
    y_bits = (gx // 4).bit_length() - 1
    for bit in range(y_bits):
        energy = summed(energy, ("gx",), lambda i, j, bit=bit: (i ^ (4 * (2 ** (bit + 1) - 1)),))
    z_bits = gy.bit_length() - 1
    for bit in range(z_bits):
        after = new_q if bit == z_bits - 1 else None
        energy = summed(energy, ("gy",), lambda i, j, bit=bit: (i ^ (1 << bit),), after)
    energy = summed(energy, ("gx", "gy"), lambda i, j: (i ^ 2, gy - 1 - j), new_p)
    energy = (jnp.sum(energy[:2], axis=1) / volume)[None, :]
    return (new_q, new_p, energy)


def solution(mesh):
    placed = (
        P("rep", None, None, "gx", "gy"),
        P("rep", None, None, "gx", "gy"),
        P("rep"),
        P("rep"),
        P(),
    )
    return jax.shard_map(
        local,
        mesh=mesh,
        in_specs=placed,
        out_specs=(
            P("rep", None, None, "gx", "gy"),
            P("rep", None, None, "gx", "gy"),
            P("rep", None),
        ),
        check_vma=False,
    )
```

```python
import functools

import jax
import jax.numpy as jnp
from jax import lax
from jax.experimental import pallas as pl
from jax.experimental.pallas import tpu as pltpu
from jax.sharding import PartitionSpec as P

LEAPS = 4
STEP = 0.05
COMPS = 4
NZ = 64
OCT = NZ // 8
WIDE = 4
LANES = 128
SITES = COMPS * NZ


def f32(*shape):
    return jax.ShapeDtypeStruct(shape, jnp.float32)


def lanes():
    return lax.broadcasted_iota(jnp.int32, (8, LANES), 1)


def rows():
    return lax.broadcasted_iota(jnp.int32, (8, LANES), 0)


def packed(load):
    octet = lanes() // 16
    out = None
    for o in range(OCT):
        moved = pltpu.roll(load(o), (16 * o + 8) % LANES, 1)
        out = moved if out is None else jnp.where(octet == o, moved, out)
    return out


def layer_of(main, edge=None):
    return (lambda c, o: main[c, 8 * o : 8 * o + 8, :], None if edge is None else (lambda c: edge[c]))


def joint(ref):
    return (lambda c, o: ref[c, 8 * o : 8 * o + 8, :], lambda c: ref[c, NZ : NZ + 8, :])


def store_main(q, p):
    def put(c, o, new_p, new_q):
        if p is not None:
            p[c, 8 * o : 8 * o + 8, :] = new_p
        if q is not None:
            q[c, 8 * o : 8 * o + 8, :] = new_q

    return put


def store_edge(q, p):
    def put(c, new_p, new_q):
        p[c, NZ : NZ + 8, :] = new_p
        q[c, NZ : NZ + 8, :] = new_q

    return put


def main_eval(down, here, up, mom, put, kap, qua, dt, energy):
    lane, row = (lanes(), rows())
    zero_lane, last_lane = (lane == 0, lane == LANES - 1)
    first_row, last_row = (row == 0, row == 7)
    nsums = {}
    for c in range(COMPS):
        cells = [here[0](c, o) for o in range(OCT)]
        edge = here[1](c)
        ghosts = [pltpu.roll(edge, (120 - 16 * o) % LANES, 1) for o in range(OCT)]
        above = [pltpu.roll(q, 7, 0) for q in cells]
        below = [pltpu.roll(q, 1, 0) for q in cells]
        left = [pltpu.roll(jnp.where(last_lane, g, q), 1, 1) for g, q in zip(ghosts, cells)]
        right = [pltpu.roll(jnp.where(zero_lane, g, q), LANES - 1, 1) for g, q in zip(ghosts, cells)]
        for o in range(OCT):
            z_up = jnp.where(last_row, above[(o + 1) % OCT], above[o])
            z_down = jnp.where(first_row, below[o - 1], below[o])
            nsums[c, o] = (down[0](c, o) + up[0](c, o)) + (left[o] + right[o]) + (z_up + z_down)
    waiting = []
    for o in range(OCT):
        cells = [here[0](c, o) for c in range(COMPS)]
        moms = [mom[0](c, o) for c in range(COMPS)]
        square = cells[0] * cells[0]
        for c in range(1, COMPS):
            square = square + cells[c] * cells[c]
        coef = (2.0 - 4.0 * qua) + (4.0 * qua) * square
        dots = None
        results = []
        for c in range(COMPS):
            q, p, nsum = (cells[c], moms[c], nsums[c, o])
            new = p + dt * ((2.0 * kap) * nsum - coef * q)
            results.append((new, q + STEP * new))
            if energy is not None:
                dots = q * nsum if dots is None else dots + q * nsum
                kin = new if energy[1] else p
                energy[0] = energy[0] + 0.5 * (kin * kin)
        if energy is not None:
            energy[0] = energy[0] + (square - kap * dots + qua * ((square - 1.0) * (square - 1.0)))
        waiting.append((o, results))
        while len(waiting) > (2 if o < OCT - 1 else 0):
            at, ready = waiting.pop(0)
            for c in range(COMPS):
                put(c, at, *ready[c])


def edge_eval(jobs, kap, qua, dt):
    lane, row = (lanes(), rows())
    slot = lane % 16
    first_row, last_row = (row == 0, row == 7)
    results = []
    for down, here, up, mom, _ in jobs:
        cells = [here[1](c) for c in range(COMPS)]
        square = cells[0] * cells[0]
        for c in range(1, COMPS):
            square = square + cells[c] * cells[c]
        coef = (2.0 - 4.0 * qua) + (4.0 * qua) * square
        for c in range(COMPS):
            q = cells[c]
            own = packed(lambda o: here[0](c, o))
            right = pltpu.roll(jnp.where(slot == 8, own, q), LANES - 1, 1)
            left = pltpu.roll(jnp.where(slot == 7, own, q), 1, 1)
            above = pltpu.roll(q, 7, 0)
            below = pltpu.roll(q, 1, 0)
            z_up = jnp.where(last_row, pltpu.roll(above, LANES - 16, 1), above)
            z_down = jnp.where(first_row, pltpu.roll(below, 16, 1), below)
            nsum = (down[1](c) + up[1](c)) + (left + right) + (z_up + z_down)
            new = mom[1](c) + dt * ((2.0 * kap) * nsum - coef * q)
            results.append((new, q + STEP * new))

    def store():
        for job, (*_, put) in enumerate(jobs):
            for c in range(COMPS):
                put(c, *results[job * COMPS + c])

    return store


def ingest_kernel(flags, field, momenta, *refs):
    mains, messages, (held, sems) = ((refs[:4], refs[4:8]), refs[8:10], refs[10:])
    copies = {
        (k, c): pltpu.make_async_copy(src.at[c], held.at[k, c], sems.at[k, c])
        for c in range(COMPS)
        for k, src in enumerate((field, momenta))
    }
    for copy in copies.values():
        copy.start()
    low = lanes() % 16 < 8
    odd = jnp.broadcast_to(flags[1], (8, LANES)) == 1
    for c in range(COMPS):
        copies[0, c].wait()
        copies[1, c].wait()
        for core in range(2):

            @pl.when(flags[0] == core)
            def _():
                for u in range(WIDE):
                    x = u if core == 0 else WIDE - 1 - u
                    packs = []
                    for k in range(2):
                        value = held[k, c, pl.ds(x, NZ, stride=WIDE), :]
                        mains[k][u][c] = value
                        packs.append(packed(lambda o: value[8 * o : 8 * o + 8, :]))
                    right = jnp.where(low, packs[0], pltpu.roll(packs[1], 8, 1))
                    left = jnp.where(low, pltpu.roll(packs[0], LANES - 8, 1), packs[1])
                    messages[0][u, c] = jnp.where(odd, left, right)
                    messages[1][u, c] = jnp.where(odd, right, left)


def ghost_kernel(flags, first, second, m1, k0, qg, pg, near, far):
    low = lanes() % 16 < 8
    odd = jnp.broadcast_to(flags[1], (8, LANES)) == 1
    for u in range(WIDE):
        for c in range(COMPS):
            left = jnp.where(odd, first[u, c], second[u, c])
            right = jnp.where(odd, second[u, c], first[u, c])
            q = jnp.where(low, left, pltpu.roll(right, 8, 1))
            p = jnp.where(low, pltpu.roll(left, LANES - 8, 1), right)
            qg[u, c] = q
            pg[u, c] = p
            if u == WIDE - 1:
                near[c] = q
    write_main(far, 0, lambda c, o: m1[c, 8 * o : 8 * o + 8, :])
    write_main(far, SITES, lambda c, o: k0[c, 8 * o : 8 * o + 8, :])
    write_edge(far, 2 * SITES, lambda c: qg[0, c])
    write_edge(far, 2 * SITES + 16, lambda c: qg[1, c])
    write_edge(far, 2 * SITES + 32, lambda c: pg[0, c])


def fresh():
    return jnp.zeros((8, LANES), jnp.float32)


def step(around, moms, outs, kap, qua, dt, energy=None, edges=True):
    spans = [around[i : i + 3] for i in range(len(moms))]
    store = None
    if edges:
        jobs = [(*span, mom, store_edge(*out)) for span, mom, out in zip(spans, moms, outs)]
        store = edge_eval(jobs, kap, qua, dt)
    for span, mom, out in zip(spans, moms, outs):
        main_eval(*span, mom, store_main(*out), kap, qua, dt, energy)
    if edges:
        store()


def inside(ref, main, edge):
    def ghosts(c):
        value = ref[edge + 8 * (c % 2) : edge + 8 * (c % 2) + 8, :]
        return value if c < 2 else pltpu.roll(value, LANES - 8, 1)

    return (lambda c, o: ref[main + NZ * c + 8 * o : main + NZ * c + 8 * o + 8, :], ghosts)


def write_main(ref, main, load):
    for c in range(COMPS):
        for o in range(OCT):
            ref[main + NZ * c + 8 * o : main + NZ * c + 8 * o + 8, :] = load(c, o)


def write_edge(ref, edge, load):
    slot = lanes() % 16
    for c in range(2):
        both = jnp.where((slot >= 4) & (slot < 12), load(c), pltpu.roll(load(c + 2), 8, 1))
        ref[edge + 8 * c : edge + 8 * c + 8, :] = both


def inner_start(
    par, far, m0, m1, m2, m3, k0, k1, k2, k3, qg, pg, near, near_g, z, zp, q1, p1, q2, p2, q3, p3, energy, msg
):
    kap, qua = (par[0], par[1])
    around = [layer_of(main, qg.at[u]) for u, main in enumerate((m0, m1, m2, m3))] + [layer_of(near, near_g)]
    total = [fresh(), False]
    held = [layer_of(mom, pg.at[u + 1]) for u, mom in enumerate((k1, k2, k3))]
    step(around, held, [(q1, p1), (q2, p2), (q3, p3)], kap, qua, 0.5 * STEP, total)
    write_main(msg, 0, joint(q1)[0])
    write_edge(msg, SITES, joint(q1)[1])
    store = store_main(z, zp)
    main_eval(layer_of(far), around[0], around[1], layer_of(k0), store, kap, qua, 0.5 * STEP, total)
    energy[...] = total[0]


def outer_first(par, beyond, far, m0, qg, pg, z, zp, q1, p1, q2, zg, n1, r1, hq, hp, nz, nzp, zpg):
    kap, qua = (par[0], par[1])
    outer, halo = (inside(beyond, 0, 2 * SITES + 16), inside(beyond, 0, 2 * SITES))
    halo = (layer_of(far)[0], halo[1])
    here = layer_of(m0, qg.at[0])

    def put(c, new_p, new_q):
        zpg[c] = new_p
        zg[c] = new_q

    edge_eval([(halo, here, (None, lambda c: qg[1, c]), (None, lambda c: pg[0, c]), put)], kap, qua, 0.5 * STEP)()
    step([outer, halo, here], [inside(beyond, SITES, 2 * SITES + 32)], [(hq, hp)], kap, qua, 0.5 * STEP)
    step([layer_of(z, zg), joint(q1), joint(q2)], [joint(p1)], [(n1, r1)], kap, qua, STEP)
    step([joint(hq), layer_of(z, zg), joint(q1)], [layer_of(zp, zpg)], [(nz, nzp)], kap, qua, STEP)


def inner_second(par, z, q1, p1, q2, p2, q3, p3, near, n1, r1, n2, r2, n3, r3, msg):
    around = [joint(z), joint(q1), joint(q2), joint(q3), joint(near)]
    moms = [joint(p1), joint(p2), joint(p3)]
    step(around, moms, [(n1, r1), (n2, r2), (n3, r3)], par[0], par[1], STEP)
    write_main(msg, 0, joint(q1)[0])
    write_edge(msg, SITES, joint(q1)[1])
    write_main(msg, SITES + 16, joint(n1)[0])


def outer_kernel(par, beyond, hq, hp, zold, zold_g, z, zp, old1, q1, p1, q2, nhq, nhp, nz, nzp, n1, r1):
    kap, qua = (par[0], par[1])
    step([inside(beyond, 0, SITES), joint(hq), layer_of(zold, zold_g)], [joint(hp)], [(nhq, nhp)], kap, qua, STEP)
    step([joint(nhq), joint(z), joint(old1)], [joint(zp)], [(nz, nzp)], kap, qua, STEP)
    step([joint(nz), joint(q1), joint(q2)], [joint(p1)], [(n1, r1)], kap, qua, STEP)


def inner_kernel(par, q1, q2, p2, q3, p3, near, n2, r2, n3, r3):
    around = [joint(q1), joint(q2), joint(q3), joint(near)]
    step(around, [joint(p2), joint(p3)], [(n2, r2), (n3, r3)], par[0], par[1], STEP)


def inner_third(par, q1, q2, p2, q3, p3, near, n2, r2, n3, r3, whole):
    inner_kernel(par, q1, q2, p2, q3, p3, near, n2, r2, n3, r3)
    for u, ref in enumerate((n2, n3)):
        for c in range(COMPS):
            whole[u, c] = ref[c, :NZ, :]


def inner_final(par, q1, q2, p2, q3, p3, near, r2, r3, energy):
    around = [joint(q1), joint(q2), joint(q3), joint(near)]
    total = [fresh(), True]
    outs = [(None, r2), (None, r3)]
    step(around, [joint(p2), joint(p3)], outs, par[0], par[1], 0.5 * STEP, total, False)
    energy[...] = total[0]


def outer_last(
    par, beyond, hq, hp, zold, z, zp, old1, q1, p1, q2, r2, r3, start, more,
    whole, energy, nhq, nhp, nz, nzp, last,
):
    kap, qua = (par[0], par[1])
    step([inside(beyond, 0, SITES), joint(hq), joint(zold)], [joint(hp)], [(nhq, nhp)], kap, qua, STEP)
    step([joint(nhq), joint(z), joint(old1)], [joint(zp)], [(nz, nzp)], kap, qua, STEP)
    store = store_main(last, None)
    outer = inside(beyond, SITES + 16, 0)
    main_eval(outer, joint(nhq), joint(z), joint(nhp), store, kap, qua, STEP, None)
    total = [more[...], True]
    store = store_main(None, whole.at[2])
    main_eval(layer_of(last), joint(nz), joint(q1), joint(nzp), store, kap, qua, 0.5 * STEP, total)
    store = store_main(None, whole.at[3])
    main_eval(joint(nz), joint(q1), joint(q2), joint(p1), store, kap, qua, 0.5 * STEP, total)
    before = jnp.sum(start[...], axis=0, keepdims=True)
    after = jnp.sum(total[0], axis=0, keepdims=True)
    row = rows()
    energy[...] = jnp.where(row == 0, before, jnp.where(row == 1, after, 0.0))
    for c in range(COMPS):
        whole[0, c] = nz[c, :NZ, :]
        whole[1, c] = q1[c, :NZ, :]
        whole[4, c] = r2[c]
        whole[5, c] = r3[c]


def place_kernel(part, flags, *refs):
    *sources, out = refs
    for core in range(2):
        for pick in range(3):

            @pl.when((flags[0] == core) & (flags[1] == pick))
            def _():
                late = sources[pick]
                for u in range(WIDE):
                    x = u if core == 0 else WIDE - 1 - u
                    for c in range(COMPS):
                        if part == 1:
                            value = late[u + 2, c]
                        else:
                            value = late[u, c] if u < 2 else sources[3 + pick][u - 2, c]
                        out[c, pl.ds(x, NZ, stride=WIDE), :] = value


def add_kernel(one, two, out):
    out[...] = one[...] + two[...]


def run(kernel, outs, scalars, arrays, scratch=(), cost=1000, held=True, raw=False, after=()):
    vmem = pl.BlockSpec(memory_space=pltpu.VMEM)
    smem = pl.BlockSpec(memory_space=pltpu.SMEM)
    place = pl.BlockSpec(memory_space=pltpu.HBM) if raw else vmem
    if held:
        outs = [pltpu.VMEM(out.shape, out.dtype) for out in outs]
    given = len(scalars) + len(arrays)

    def body(*refs):
        kernel(*refs[:given], *refs[given + len(after) :])

    return pl.pallas_call(
        body,
        out_shape=outs,
        in_specs=[smem] * len(scalars) + [place] * len(arrays) + [pl.BlockSpec(memory_space=pl.ANY)] * len(after),
        out_specs=[vmem] * len(outs),
        scratch_shapes=list(scratch),
        cost_estimate=pl.CostEstimate(flops=cost * 4, bytes_accessed=cost, transcendentals=0),
        compiler_params=pltpu.CompilerParams(vmem_limit_bytes=12 * 1024 * 1024),
    )(*scalars, *arrays, *after)


def pair_swap(value, axis, other):
    return lax.ppermute(value, axis, [(i, other(i)) for i in range(lax.axis_size(axis)) if other(i) is not None])


def local(field, momenta, kappa, quartic, acceptance):
    gx, gy, reps = (lax.axis_size("gx"), lax.axis_size("gy"), lax.axis_size("rep"))
    volume = NZ * WIDE * LANES * gx * gy
    core = lax.axis_index("gx") % 2
    flags = jnp.stack([core, lax.axis_index("gy") % 2]).astype(jnp.int32)
    position = lax.axis_index("rep")
    partner = acceptance[position]
    pick = jnp.where(partner == position, 0, jnp.where(partner == position ^ 1, 1, 2))
    choice = jnp.stack([core, pick]).astype(jnp.int32)
    par = jnp.concatenate([kappa, quartic])

    def far(value):
        return pair_swap(value, "gx", lambda i: (i + 1) % gx if i % 2 == 1 else (i - 1) % gx)

    def near(value):
        return pair_swap(value, "gx", lambda i: i ^ 1)

    def beside(value, parity):
        return pair_swap(value, "gy", lambda i: (i + 1) % gy if i % 2 == parity else (i - 1) % gy)

    def exchanged(value):
        first = pair_swap(value, "rep", lambda i: i ^ 1 if i ^ 1 < reps else None)
        second = pair_swap(value, "rep", lambda i: ((i - 1) ^ 1) + 1 if 0 < i and ((i - 1) ^ 1) + 1 < reps else None)
        return (first, second)

    main, both = (f32(COMPS, NZ, LANES), f32(COMPS, NZ + 8, LANES))
    edges, whole, vreg = (f32(WIDE, COMPS, 8, LANES), f32(WIDE, COMPS, NZ, LANES), f32(8, LANES))
    edge = f32(COMPS, 8, LANES)

    m0, m1, m2, m3, k0, k1, k2, k3, to_first, to_second = run(
        ingest_kernel,
        [main] * 8 + [edges] * 2,
        [flags],
        [
            pltpu.with_memory_space_constraint(value.reshape(COMPS, NZ * WIDE, LANES), pltpu.HBM)
            for value in (field, momenta)
        ],
        scratch=[pltpu.VMEM((2, COMPS, NZ * WIDE, LANES), jnp.float32), pltpu.SemaphoreType.DMA((2, COMPS))],
        raw=True,
    )
    far0, near0 = (far(m0), near(m3))
    first, second = (beside(to_first, 0), beside(to_second, 1))
    qg, pg, near_g, to_far = run(
        ghost_kernel, [edges, edges, edge, f32(2 * SITES + 80, LANES)], [flags], [first, second, m1, k0]
    )
    near_ghost, beyond0 = (near(near_g), far(to_far))
    z1, zp1, a1, b1, a2, b2, a3, b3, start, msg = run(
        inner_start,
        [main, main] + [both] * 6 + [vreg, f32(SITES + 32, LANES)],
        [par],
        [far0, m0, m1, m2, m3, k0, k1, k2, k3, qg, pg, near0, near_ghost],
    )
    beyond1, near1 = (far(msg), near(a3))
    c2, d2, c3, d3 = run(inner_kernel, [both] * 4, [par], [a1, a2, b2, a3, b3, near1], after=[choice])
    near2 = near(c3)
    zg1, c1, d1, hq1, hp1, z2, zp2 = run(
        outer_first,
        [edge] + [both] * 6,
        [par],
        [beyond0, far0, m0, qg, pg, z1, zp1, a1, b1, a2],
        scratch=[pltpu.VMEM((COMPS, 8, LANES), jnp.float32)],
    )
    e1, f1, e2, f2, e3, f3, msg = run(
        inner_second,
        [both] * 6 + [f32(2 * SITES + 16, LANES)],
        [par],
        [z2, c1, d1, c2, d2, c3, d3, near2],
    )
    beyond2 = far(msg)
    near3 = near(e3)
    hq2, hp2, z3, zp3, g1, h1 = run(
        outer_kernel,
        [both] * 6,
        [par],
        [beyond1, hq1, hp1, z1, zg1, z2, zp2, c1, e1, f1, e2],
    )
    g2, h2, g3, h3, early = run(
        inner_third,
        [both] * 4 + [f32(2, COMPS, NZ, LANES)],
        [par],
        [e1, e2, f2, e3, f3, near3],
        after=[hq2],
    )
    near4 = near(g3)
    first_early, second_early = exchanged(early)
    r2, r3, more = run(inner_final, [main, main, vreg], [par], [g1, g2, h2, g3, h3, near4])
    late, energy = run(
        outer_last,
        [f32(6, COMPS, NZ, LANES), vreg],
        [par],
        [beyond2, hq2, hp2, z2, z3, zp3, e1, g1, h1, g2, r2, r3, start, more],
        after=[first_early, second_early],
        scratch=[pltpu.VMEM((COMPS, NZ + 8, LANES), jnp.float32)] * 4 + [pltpu.VMEM((COMPS, NZ, LANES), jnp.float32)],
    )
    first_late, second_late = exchanged(late)

    def placed(part, arrays):
        kernel = functools.partial(place_kernel, part)
        return run(kernel, [f32(COMPS, NZ * WIDE, LANES)], [choice], arrays, held=False)[0].reshape(field.shape)

    def summed(value, axes, other, after=None):
        sizes = [lax.axis_size(axis) for axis in axes]
        pairs = []
        for i in range(sizes[0]):
            for j in range(sizes[1] if len(axes) > 1 else 1):
                to = other(i, j)
                pairs.append((i, to[0]) if len(axes) == 1 else (i * sizes[1] + j, to[0] * sizes[1] + to[1]))
        got = lax.ppermute(value, axes, pairs)
        if after is None:
            return value + got
        later = pltpu.with_memory_space_constraint(after, pltpu.HBM)
        return run(add_kernel, [vreg], [], [value, got], after=[later])[0]

    new_q = placed(0, [late, first_late, second_late, early, first_early, second_early])
    new_p = placed(1, [late, first_late, second_late])
    energy = energy + near(energy)
    y_bits = (gx // 4).bit_length() - 1
    for bit in range(y_bits):
        energy = summed(energy, ("gx",), lambda i, j, bit=bit: (i ^ (4 * (2 ** (bit + 1) - 1)),))
    z_bits = gy.bit_length() - 1
    for bit in range(z_bits):
        after = new_q if bit == z_bits - 1 else None
        energy = summed(energy, ("gy",), lambda i, j, bit=bit: (i ^ (1 << bit),), after)
    energy = summed(energy, ("gx", "gy"), lambda i, j: (i ^ 2, gy - 1 - j), new_p)
    energy = (jnp.sum(energy[:2], axis=1) / volume)[None, :]
    return (new_q, new_p, energy)


def solution(mesh):
    placed = (
        P("rep", None, None, "gx", "gy"),
        P("rep", None, None, "gx", "gy"),
        P("rep"),
        P("rep"),
        P(),
    )
    return jax.shard_map(
        local,
        mesh=mesh,
        in_specs=placed,
        out_specs=(
            P("rep", None, None, "gx", "gy"),
            P("rep", None, None, "gx", "gy"),
            P("rep", None),
        ),
        check_vma=False,
    )
```

```python
import functools

import jax
import jax.numpy as jnp
from jax import lax
from jax.experimental import pallas as pl
from jax.experimental.pallas import tpu as pltpu
from jax.sharding import PartitionSpec as P

LEAPS = 4
STEP = 0.05
COMPS = 4
NZ = 64
OCT = NZ // 8
WIDE = 4
LANES = 128
SITES = COMPS * NZ


def f32(*shape):
    return jax.ShapeDtypeStruct(shape, jnp.float32)


def lanes():
    return lax.broadcasted_iota(jnp.int32, (8, LANES), 1)


def rows():
    return lax.broadcasted_iota(jnp.int32, (8, LANES), 0)


def packed(load):
    octet = lanes() // 16
    out = None
    for o in range(OCT):
        moved = pltpu.roll(load(o), (16 * o + 8) % LANES, 1)
        out = moved if out is None else jnp.where(octet == o, moved, out)
    return out


def layer_of(main, edge=None):
    return (lambda c, o: main[c, 8 * o : 8 * o + 8, :], None if edge is None else (lambda c: edge[c]))


def joint(ref):
    return (lambda c, o: ref[c, 8 * o : 8 * o + 8, :], lambda c: ref[c, NZ : NZ + 8, :])


def store_main(q, p):
    def put(c, o, new_p, new_q):
        if p is not None:
            p[c, 8 * o : 8 * o + 8, :] = new_p
        if q is not None:
            q[c, 8 * o : 8 * o + 8, :] = new_q

    return put


def store_edge(q, p):
    def put(c, new_p, new_q):
        p[c, NZ : NZ + 8, :] = new_p
        q[c, NZ : NZ + 8, :] = new_q

    return put


def settings(ref):
    row = lax.broadcasted_iota(jnp.int32, (LANES, LANES), 0)
    lane = lax.broadcasted_iota(jnp.int32, (LANES, LANES), 1)
    mix = jnp.where(jnp.abs(row - lane) == 1, 1.0, 0.0).astype(jnp.bfloat16)
    return (ref[0], ref[1], jnp.concatenate([mix, mix], axis=0))


def main_eval(down, here, up, mom, put, par, dt, energy):
    kap, qua, mix = par
    lane, row = (lanes(), rows())
    zero_lane, last_lane = (lane == 0, lane == LANES - 1)
    first_row, last_row = (row == 0, row == 7)
    nsums = {}
    for c in range(COMPS):
        cells = [here[0](c, o) for o in range(OCT)]
        edge = here[1](c)
        whole = jnp.concatenate(cells, axis=0)
        high = whole.astype(jnp.bfloat16)
        low = (whole - high.astype(jnp.float32)).astype(jnp.bfloat16)
        beside = jnp.dot(jnp.concatenate([high, low], axis=1), mix, preferred_element_type=jnp.float32)
        left = [pltpu.roll(edge, (121 - 16 * o) % LANES, 1) for o in range(OCT)]
        right = [pltpu.roll(edge, (119 - 16 * o) % LANES, 1) for o in range(OCT)]
        above = [pltpu.roll(q, 7, 0) for q in cells]
        below = [pltpu.roll(q, 1, 0) for q in cells]
        for o in range(OCT):
            z_up = jnp.where(last_row, above[(o + 1) % OCT], above[o])
            z_down = jnp.where(first_row, below[o - 1], below[o])
            ghost = jnp.where(zero_lane, left[o], jnp.where(last_lane, right[o], 0.0))
            y_sum = beside[8 * o : 8 * o + 8] + ghost
            nsums[c, o] = (down[0](c, o) + up[0](c, o)) + y_sum + (z_up + z_down)
    waiting = []
    for o in range(OCT):
        cells = [here[0](c, o) for c in range(COMPS)]
        moms = [mom[0](c, o) for c in range(COMPS)]
        square = cells[0] * cells[0]
        for c in range(1, COMPS):
            square = square + cells[c] * cells[c]
        coef = (2.0 - 4.0 * qua) + (4.0 * qua) * square
        dots = None
        results = []
        for c in range(COMPS):
            q, p, nsum = (cells[c], moms[c], nsums[c, o])
            new = p + dt * ((2.0 * kap) * nsum - coef * q)
            results.append((new, q + STEP * new))
            if energy is not None:
                dots = q * nsum if dots is None else dots + q * nsum
                kin = new if energy[1] else p
                energy[0] = energy[0] + 0.5 * (kin * kin)
        if energy is not None:
            energy[0] = energy[0] + (square - kap * dots + qua * ((square - 1.0) * (square - 1.0)))
        waiting.append((o, results))
        while len(waiting) > (2 if o < OCT - 1 else 0):
            at, ready = waiting.pop(0)
            for c in range(COMPS):
                put(c, at, *ready[c])


def edge_eval(jobs, par, dt):
    kap, qua, _ = par
    lane, row = (lanes(), rows())
    slot = lane % 16
    first_row, last_row = (row == 0, row == 7)
    results = []
    for down, here, up, mom, _ in jobs:
        cells = [here[1](c) for c in range(COMPS)]
        square = cells[0] * cells[0]
        for c in range(1, COMPS):
            square = square + cells[c] * cells[c]
        coef = (2.0 - 4.0 * qua) + (4.0 * qua) * square
        for c in range(COMPS):
            q = cells[c]
            own = packed(lambda o: here[0](c, o))
            right = pltpu.roll(jnp.where(slot == 8, own, q), LANES - 1, 1)
            left = pltpu.roll(jnp.where(slot == 7, own, q), 1, 1)
            above = pltpu.roll(q, 7, 0)
            below = pltpu.roll(q, 1, 0)
            z_up = jnp.where(last_row, pltpu.roll(above, LANES - 16, 1), above)
            z_down = jnp.where(first_row, pltpu.roll(below, 16, 1), below)
            nsum = (down[1](c) + up[1](c)) + (left + right) + (z_up + z_down)
            new = mom[1](c) + dt * ((2.0 * kap) * nsum - coef * q)
            results.append((new, q + STEP * new))

    def store():
        for job, (*_, put) in enumerate(jobs):
            for c in range(COMPS):
                put(c, *results[job * COMPS + c])

    return store


def ingest_kernel(flags, field, momenta, *refs):
    mains, messages, (held, sems) = ((refs[:4], refs[4:8]), refs[8:10], refs[10:])
    copies = {
        (k, c): pltpu.make_async_copy(src.at[c], held.at[k, c], sems.at[k, c])
        for c in range(COMPS)
        for k, src in enumerate((field, momenta))
    }
    for copy in copies.values():
        copy.start()
    low = lanes() % 16 < 8
    odd = flags[1] == 1
    mirrored = jnp.broadcast_to(flags[0, :1, :], (NZ, LANES)) == 1
    for c in range(COMPS):
        copies[0, c].wait()
        copies[1, c].wait()
        lines = [[held[k, c, pl.ds(x, NZ, stride=WIDE), :] for x in range(WIDE)] for k in range(2)]
        for u in range(WIDE):
            packs = []
            for k in range(2):
                value = jnp.where(mirrored, lines[k][WIDE - 1 - u], lines[k][u])
                mains[k][u][c] = value
                packs.append(packed(lambda o: value[8 * o : 8 * o + 8, :]))
            right = jnp.where(low, packs[0], pltpu.roll(packs[1], 8, 1))
            left = jnp.where(low, pltpu.roll(packs[0], LANES - 8, 1), packs[1])
            messages[0][u, c] = jnp.where(odd, left, right)
            messages[1][u, c] = jnp.where(odd, right, left)


def ghost_kernel(flags, first, second, m1, k0, qg, pg, near, far):
    low = lanes() % 16 < 8
    odd = flags[1] == 1
    for u in range(WIDE):
        for c in range(COMPS):
            left = jnp.where(odd, first[u, c], second[u, c])
            right = jnp.where(odd, second[u, c], first[u, c])
            q = jnp.where(low, left, pltpu.roll(right, 8, 1))
            p = jnp.where(low, pltpu.roll(left, LANES - 8, 1), right)
            qg[u, c] = q
            pg[u, c] = p
            if u == WIDE - 1:
                near[c] = q
    write_main(far, 0, lambda c, o: m1[c, 8 * o : 8 * o + 8, :])
    write_main(far, SITES, lambda c, o: k0[c, 8 * o : 8 * o + 8, :])
    write_edge(far, 2 * SITES, lambda c: qg[0, c])
    write_edge(far, 2 * SITES + 16, lambda c: qg[1, c])
    write_edge(far, 2 * SITES + 32, lambda c: pg[0, c])


def fresh():
    return jnp.zeros((8, LANES), jnp.float32)


def step(around, moms, outs, par, dt, energy=None, edges=True):
    spans = [around[i : i + 3] for i in range(len(moms))]
    store = None
    if edges:
        jobs = [(*span, mom, store_edge(*out)) for span, mom, out in zip(spans, moms, outs)]
        store = edge_eval(jobs, par, dt)
    for span, mom, out in zip(spans, moms, outs):
        main_eval(*span, mom, store_main(*out), par, dt, energy)
    if edges:
        store()


def inside(ref, main, edge):
    def ghosts(c):
        value = ref[edge + 8 * (c % 2) : edge + 8 * (c % 2) + 8, :]
        return value if c < 2 else pltpu.roll(value, LANES - 8, 1)

    return (lambda c, o: ref[main + NZ * c + 8 * o : main + NZ * c + 8 * o + 8, :], ghosts)


def write_main(ref, main, load):
    for c in range(COMPS):
        for o in range(OCT):
            ref[main + NZ * c + 8 * o : main + NZ * c + 8 * o + 8, :] = load(c, o)


def write_edge(ref, edge, load):
    slot = lanes() % 16
    for c in range(2):
        both = jnp.where((slot >= 4) & (slot < 12), load(c), pltpu.roll(load(c + 2), 8, 1))
        ref[edge + 8 * c : edge + 8 * c + 8, :] = both


def inner_start(
    par, far, m0, m1, m2, m3, k0, k1, k2, k3, qg, pg, near, near_g, z, zp, q1, p1, q2, p2, q3, p3, energy, msg, msg_near
):
    par = settings(par)
    around = [layer_of(main, qg.at[u]) for u, main in enumerate((m0, m1, m2, m3))] + [layer_of(near, near_g)]
    total = [fresh(), False]
    held = [layer_of(mom, pg.at[u + 1]) for u, mom in enumerate((k1, k2, k3))]
    step(around, held, [(q1, p1), (q2, p2), (q3, p3)], par, 0.5 * STEP, total)
    write_main(msg, 0, joint(q1)[0])
    write_edge(msg, SITES, joint(q1)[1])
    write_main(msg_near, 0, joint(q3)[0])
    write_edge(msg_near, SITES, joint(q3)[1])
    store = store_main(z, zp)
    main_eval(layer_of(far), around[0], around[1], layer_of(k0), store, par, 0.5 * STEP, total)
    energy[...] = total[0]


def outer_first(par, beyond, far, m0, qg, pg, z, zp, q1, p1, q2, zg, n1, r1, hq, hp, nz, nzp, zpg):
    par = settings(par)
    outer, halo = (inside(beyond, 0, 2 * SITES + 16), inside(beyond, 0, 2 * SITES))
    halo = (layer_of(far)[0], halo[1])
    here = layer_of(m0, qg.at[0])

    def put(c, new_p, new_q):
        zpg[c] = new_p
        zg[c] = new_q

    edge_eval([(halo, here, (None, lambda c: qg[1, c]), (None, lambda c: pg[0, c]), put)], par, 0.5 * STEP)()
    step([outer, halo, here], [inside(beyond, SITES, 2 * SITES + 32)], [(hq, hp)], par, 0.5 * STEP)
    step([layer_of(z, zg), joint(q1), joint(q2)], [joint(p1)], [(n1, r1)], par, STEP)
    step([joint(hq), layer_of(z, zg), joint(q1)], [layer_of(zp, zpg)], [(nz, nzp)], par, STEP)


def inner_second(par, z, q1, p1, q2, p2, q3, p3, near, n1, r1, n2, r2, n3, r3, msg, msg_near):
    around = [joint(z), joint(q1), joint(q2), joint(q3), inside(near, 0, SITES)]
    moms = [joint(p1), joint(p2), joint(p3)]
    step(around, moms, [(n1, r1), (n2, r2), (n3, r3)], settings(par), STEP)
    write_main(msg, 0, joint(q1)[0])
    write_edge(msg, SITES, joint(q1)[1])
    write_main(msg, SITES + 16, joint(n1)[0])
    write_main(msg_near, 0, joint(n3)[0])
    write_edge(msg_near, SITES, joint(n3)[1])


def outer_kernel(par, beyond, hq, hp, zold, zold_g, z, zp, old1, q1, p1, q2, nhq, nhp, nz, nzp, n1, r1):
    par = settings(par)
    step([inside(beyond, 0, SITES), joint(hq), layer_of(zold, zold_g)], [joint(hp)], [(nhq, nhp)], par, STEP)
    step([joint(nhq), joint(z), joint(old1)], [joint(zp)], [(nz, nzp)], par, STEP)
    step([joint(nz), joint(q1), joint(q2)], [joint(p1)], [(n1, r1)], par, STEP)


def inner_kernel(par, q1, q2, p2, q3, p3, near, n2, r2, n3, r3, msg):
    around = [joint(q1), joint(q2), joint(q3), inside(near, 0, SITES)]
    step(around, [joint(p2), joint(p3)], [(n2, r2), (n3, r3)], settings(par), STEP)
    write_main(msg, 0, joint(n3)[0])
    write_edge(msg, SITES, joint(n3)[1])


def inner_third(par, q1, q2, p2, q3, p3, near, n2, r2, n3, r3, msg, whole):
    around = [joint(q1), joint(q2), joint(q3), inside(near, 0, SITES)]
    step(around, [joint(p2), joint(p3)], [(n2, r2), (n3, r3)], settings(par), STEP)
    write_main(msg, 0, joint(n3)[0])
    for u, ref in enumerate((n2, n3)):
        for c in range(COMPS):
            whole[u, c] = ref[c, :NZ, :]


def inner_final(par, q1, q2, p2, q3, p3, near, r2, r3, energy):
    around = [joint(q1), joint(q2), joint(q3), inside(near, 0, 0)]
    total = [fresh(), True]
    outs = [(None, r2), (None, r3)]
    step(around, [joint(p2), joint(p3)], outs, settings(par), 0.5 * STEP, total, False)
    energy[...] = total[0]


def outer_last(
    par, beyond, hq, hp, zold, z, zp, old1, q1, p1, q2, r2, r3, start, more,
    whole, energy, nhq, nhp, nz, nzp, last,
):
    par = settings(par)
    step([inside(beyond, 0, SITES), joint(hq), joint(zold)], [joint(hp)], [(nhq, nhp)], par, STEP)
    step([joint(nhq), joint(z), joint(old1)], [joint(zp)], [(nz, nzp)], par, STEP)
    store = store_main(last, None)
    outer = inside(beyond, SITES + 16, 0)
    main_eval(outer, joint(nhq), joint(z), joint(nhp), store, par, STEP, None)
    total = [more[...], True]
    store = store_main(None, whole.at[2])
    main_eval(layer_of(last), joint(nz), joint(q1), joint(nzp), store, par, 0.5 * STEP, total)
    store = store_main(None, whole.at[3])
    main_eval(joint(nz), joint(q1), joint(q2), joint(p1), store, par, 0.5 * STEP, total)
    before = jnp.sum(start[...], axis=0, keepdims=True)
    after = jnp.sum(total[0], axis=0, keepdims=True)
    row = rows()
    energy[...] = jnp.where(row == 0, before, jnp.where(row == 1, after, 0.0))
    for c in range(COMPS):
        whole[0, c] = nz[c, :NZ, :]
        whole[1, c] = q1[c, :NZ, :]
        whole[4, c] = r2[c]
        whole[5, c] = r3[c]


def place_kernel(choice, *refs):
    late, early, (new_q, new_p, held, sems) = (refs[:3], refs[3:6], refs[6:])
    mirrored, first, second = (jnp.broadcast_to(choice[i, :1, :], (NZ, LANES)) == 1 for i in range(3))

    def picked(sources, u, c):
        return jnp.where(first, sources[1][u, c], jnp.where(second, sources[2][u, c], sources[0][u, c]))

    copies = []
    for k, out in enumerate((new_q, new_p)):
        for c in range(COMPS):
            if k == 1:
                layers = [picked(late, u + 2, c) for u in range(WIDE)]
            else:
                layers = [picked(late, u, c) if u < 2 else picked(early, u - 2, c) for u in range(WIDE)]
            for x in range(WIDE):
                value = jnp.where(mirrored, layers[WIDE - 1 - x], layers[x])
                held[k, c, pl.ds(x, NZ, stride=WIDE), :] = value
            copies.append(pltpu.make_async_copy(held.at[k, c], out.at[c], sems.at[k, c]))
            copies[-1].start()
    for copy in copies:
        copy.wait()


def add_kernel(*refs):
    *parts, out = refs
    out[...] = sum((ref[...] for ref in parts[1:]), parts[0][...])


def run(kernel, outs, arrays, scratch=(), raw=(), after=(), held=True):
    vmem, hbm = (pl.BlockSpec(memory_space=pltpu.VMEM), pl.BlockSpec(memory_space=pltpu.HBM))
    given = len(arrays) + len(raw)

    def body(*refs):
        kernel(*refs[:given], *refs[given + len(after) :])

    space = pltpu.VMEM if held else pltpu.HBM
    return pl.pallas_call(
        body,
        out_shape=[space(out.shape, out.dtype) for out in outs],
        in_specs=[vmem] * len(arrays) + [hbm] * len(raw) + [pl.BlockSpec(memory_space=pl.ANY)] * len(after),
        out_specs=[vmem if held else hbm] * len(outs),
        scratch_shapes=list(scratch),
        cost_estimate=pl.CostEstimate(flops=4000, bytes_accessed=1000, transcendentals=0),
        compiler_params=pltpu.CompilerParams(vmem_limit_bytes=12 * 1024 * 1024),
    )(
        *(pltpu.with_memory_space_constraint(value, pltpu.VMEM) for value in arrays),
        *(pltpu.with_memory_space_constraint(value, pltpu.HBM) for value in raw),
        *after,
    )


def pair_swap(value, axis, other):
    return lax.ppermute(value, axis, [(i, other(i)) for i in range(lax.axis_size(axis)) if other(i) is not None])


def local(field, momenta, kappa, quartic, acceptance):
    gx, gy, reps = (lax.axis_size("gx"), lax.axis_size("gy"), lax.axis_size("rep"))
    volume = NZ * WIDE * LANES * gx * gy
    core = lax.axis_index("gx") % 2
    spread = lambda values: jnp.broadcast_to(jnp.stack(values)[:, None, None], (len(values), 8, LANES))
    flags = spread([core, lax.axis_index("gy") % 2]).astype(jnp.int32)
    position = lax.axis_index("rep")
    partner = acceptance[position]
    first, second = (partner == position ^ 1, (partner != position) & (partner != position ^ 1))
    choice = spread([core, first.astype(core.dtype), second.astype(core.dtype)]).astype(jnp.int32)
    par = spread([kappa[0], quartic[0]])

    def far(value):
        return pair_swap(value, "gx", lambda i: (i + 1) % gx if i % 2 == 1 else (i - 1) % gx)

    def near(value):
        return pair_swap(value, "gx", lambda i: i ^ 1)

    def beside(value, parity):
        return pair_swap(value, "gy", lambda i: (i + 1) % gy if i % 2 == parity else (i - 1) % gy)

    def exchanged(value):
        first = pair_swap(value, "rep", lambda i: i ^ 1 if i ^ 1 < reps else None)
        second = pair_swap(value, "rep", lambda i: ((i - 1) ^ 1) + 1 if 0 < i and ((i - 1) ^ 1) + 1 < reps else None)
        return (first, second)

    main, both = (f32(COMPS, NZ, LANES), f32(COMPS, NZ + 8, LANES))
    edges, whole, vreg = (f32(WIDE, COMPS, 8, LANES), f32(WIDE, COMPS, NZ, LANES), f32(8, LANES))
    edge, side = (f32(COMPS, 8, LANES), f32(SITES + 16, LANES))

    m0, m1, m2, m3, k0, k1, k2, k3, to_first, to_second = run(
        ingest_kernel,
        [main] * 8 + [edges] * 2,
        [flags],
        scratch=[pltpu.VMEM((2, COMPS, NZ * WIDE, LANES), jnp.float32), pltpu.SemaphoreType.DMA((2, COMPS))],
        raw=[value.reshape(COMPS, NZ * WIDE, LANES) for value in (field, momenta)],
    )
    far0, near0 = (far(m0), near(m3))
    first, second = (beside(to_first, 0), beside(to_second, 1))
    qg, pg, near_g, to_far = run(
        ghost_kernel, [edges, edges, edge, f32(2 * SITES + 48, LANES)], [flags, first, second, m1, k0]
    )
    near_ghost, beyond0 = (near(near_g), far(to_far))
    z1, zp1, a1, b1, a2, b2, a3, b3, start, msg, to_near = run(
        inner_start,
        [main, main] + [both] * 6 + [vreg, f32(SITES + 24, LANES), side],
        [par, far0, m0, m1, m2, m3, k0, k1, k2, k3, qg, pg, near0, near_ghost],
    )
    beyond1, near1 = (far(msg), near(to_near))
    arrays = [par, a1, a2, b2, a3, b3, near1]
    c2, d2, c3, d3, to_near = run(inner_kernel, [both] * 4 + [side], arrays, after=[choice])
    near2 = near(to_near)
    zg1, c1, d1, hq1, hp1, z2, zp2 = run(
        outer_first,
        [edge] + [both] * 6,
        [par, beyond0, far0, m0, qg, pg, z1, zp1, a1, b1, a2],
        scratch=[pltpu.VMEM((COMPS, 8, LANES), jnp.float32)],
    )
    e1, f1, e2, f2, e3, f3, msg, to_near = run(
        inner_second,
        [both] * 6 + [f32(2 * SITES + 16, LANES), side],
        [par, z2, c1, d1, c2, d2, c3, d3, near2],
    )
    beyond2 = far(msg)
    near3 = near(to_near)
    hq2, hp2, z3, zp3, g1, h1 = run(
        outer_kernel,
        [both] * 6,
        [par, beyond1, hq1, hp1, z1, zg1, z2, zp2, c1, e1, f1, e2],
    )
    g2, h2, g3, h3, to_near, early = run(
        inner_third,
        [both] * 4 + [f32(SITES, LANES), f32(2, COMPS, NZ, LANES)],
        [par, e1, e2, f2, e3, f3, near3],
        after=[beyond1],
    )
    near4 = near(to_near)
    first_early, second_early = exchanged(early)
    r2, r3, more = run(inner_final, [main, main, vreg], [par, g1, g2, h2, g3, h3, near4])
    late, energy = run(
        outer_last,
        [f32(6, COMPS, NZ, LANES), vreg],
        [par, beyond2, hq2, hp2, z2, z3, zp3, e1, g1, h1, g2, r2, r3, start, more],
        after=[first_early, second_early],
        scratch=[pltpu.VMEM((COMPS, NZ + 8, LANES), jnp.float32)] * 4 + [pltpu.VMEM((COMPS, NZ, LANES), jnp.float32)],
    )
    first_late, second_late = exchanged(late)

    new_q, new_p = run(
        place_kernel,
        [f32(COMPS, NZ * WIDE, LANES)] * 2,
        [choice, late, first_late, second_late, early, first_early, second_early],
        scratch=[pltpu.VMEM((2, COMPS, NZ * WIDE, LANES), jnp.float32), pltpu.SemaphoreType.DMA((2, COMPS))],
        held=False,
    )
    energy = energy + near(energy)
    moved = [pair_swap(energy, "gx", lambda i, k=k: i ^ (4 * k)) for k in range(1, gx // 4)]
    energy = sum(moved, energy)
    energy = energy + pair_swap(energy, "gy", lambda i: i ^ 1)

    def across(i_bit, j_bit):
        pairs = [(i * gy + j, (i ^ i_bit) * gy + (j ^ j_bit)) for i in range(gx) for j in range(gy)]
        return lax.ppermute(energy, ("gx", "gy"), pairs)

    parts = [energy, across(0, 2), across(2, 2), across(2, 1)]
    placed_first = [pltpu.with_memory_space_constraint(value, pltpu.HBM) for value in (new_q, new_p)]
    (energy,) = run(add_kernel, [vreg], parts, after=placed_first)
    energy = (jnp.sum(energy[:2], axis=1) / volume)[None, :]
    return (new_q.reshape(field.shape), new_p.reshape(field.shape), energy)


def solution(mesh):
    placed = (
        P("rep", None, None, "gx", "gy"),
        P("rep", None, None, "gx", "gy"),
        P("rep"),
        P("rep"),
        P(),
    )
    return jax.shard_map(
        local,
        mesh=mesh,
        in_specs=placed,
        out_specs=(
            P("rep", None, None, "gx", "gy"),
            P("rep", None, None, "gx", "gy"),
            P("rep", None),
        ),
        check_vma=False,
    )
```

```python
import functools

import jax
import jax.numpy as jnp
from jax import lax
from jax.experimental import pallas as pl
from jax.experimental.pallas import tpu as pltpu
from jax.sharding import PartitionSpec as P

LEAPS = 4
STEP = 0.05
COMPS = 4
NZ = 64
OCT = NZ // 8
WIDE = 4
LANES = 128
SITES = COMPS * NZ


def f32(*shape):
    return jax.ShapeDtypeStruct(shape, jnp.float32)


def lanes():
    return lax.broadcasted_iota(jnp.int32, (8, LANES), 1)


def rows():
    return lax.broadcasted_iota(jnp.int32, (8, LANES), 0)


def packed(load):
    octet = lanes() // 16
    out = None
    for o in range(OCT):
        moved = pltpu.roll(load(o), (16 * o + 8) % LANES, 1)
        out = moved if out is None else jnp.where(octet == o, moved, out)
    return out


def layer_of(main, edge=None):
    return (lambda c, o: main[c, 8 * o : 8 * o + 8, :], None if edge is None else (lambda c: edge[c]))


def joint(ref):
    return (lambda c, o: ref[c, 8 * o : 8 * o + 8, :], lambda c: ref[c, NZ : NZ + 8, :])


def store_main(q, p):
    def put(c, o, new_p, new_q):
        if p is not None:
            p[c, 8 * o : 8 * o + 8, :] = new_p
        if q is not None:
            q[c, 8 * o : 8 * o + 8, :] = new_q

    return put


def store_edge(q, p):
    def put(c, new_p, new_q):
        p[c, NZ : NZ + 8, :] = new_p
        q[c, NZ : NZ + 8, :] = new_q

    return put


def settings(ref):
    row = lax.broadcasted_iota(jnp.int32, (LANES, LANES), 0)
    lane = lax.broadcasted_iota(jnp.int32, (LANES, LANES), 1)
    mix = jnp.where(jnp.abs(row - lane) == 1, 1.0, 0.0).astype(jnp.bfloat16)
    return (ref[0], ref[1], jnp.concatenate([mix, mix], axis=0))


def main_eval(down, here, up, mom, put, par, dt, energy):
    kap, qua, mix = par
    lane, row = (lanes(), rows())
    zero_lane, last_lane = (lane == 0, lane == LANES - 1)
    first_row, last_row = (row == 0, row == 7)
    nsums = {}
    for c in range(COMPS):
        cells = [here[0](c, o) for o in range(OCT)]
        edge = here[1](c)
        whole = jnp.concatenate(cells, axis=0)
        high = whole.astype(jnp.bfloat16)
        low = (whole - high.astype(jnp.float32)).astype(jnp.bfloat16)
        beside = jnp.dot(jnp.concatenate([high, low], axis=1), mix, preferred_element_type=jnp.float32)
        left = [pltpu.roll(edge, (121 - 16 * o) % LANES, 1) for o in range(OCT)]
        right = [pltpu.roll(edge, (119 - 16 * o) % LANES, 1) for o in range(OCT)]
        above = [pltpu.roll(q, 7, 0) for q in cells]
        below = [pltpu.roll(q, 1, 0) for q in cells]
        for o in range(OCT):
            z_up = jnp.where(last_row, above[(o + 1) % OCT], above[o])
            z_down = jnp.where(first_row, below[o - 1], below[o])
            ghost = jnp.where(zero_lane, left[o], jnp.where(last_lane, right[o], 0.0))
            y_sum = beside[8 * o : 8 * o + 8] + ghost
            nsums[c, o] = (down[0](c, o) + up[0](c, o)) + y_sum + (z_up + z_down)
    waiting = []
    for o in range(OCT):
        cells = [here[0](c, o) for c in range(COMPS)]
        moms = [mom[0](c, o) for c in range(COMPS)]
        square = cells[0] * cells[0]
        for c in range(1, COMPS):
            square = square + cells[c] * cells[c]
        coef = (2.0 - 4.0 * qua) + (4.0 * qua) * square
        dots = None
        results = []
        for c in range(COMPS):
            q, p, nsum = (cells[c], moms[c], nsums[c, o])
            new = p + dt * ((2.0 * kap) * nsum - coef * q)
            results.append((new, q + STEP * new))
            if energy is not None:
                dots = q * nsum if dots is None else dots + q * nsum
                kin = new if energy[1] else p
                energy[0] = energy[0] + 0.5 * (kin * kin)
        if energy is not None:
            energy[0] = energy[0] + (square - kap * dots + qua * ((square - 1.0) * (square - 1.0)))
        waiting.append((o, results))
        while len(waiting) > (2 if o < OCT - 1 else 0):
            at, ready = waiting.pop(0)
            for c in range(COMPS):
                put(c, at, *ready[c])


def edge_eval(jobs, par, dt):
    kap, qua, _ = par
    lane, row = (lanes(), rows())
    slot = lane % 16
    first_row, last_row = (row == 0, row == 7)
    results = []
    for down, here, up, mom, _ in jobs:
        cells = [here[1](c) for c in range(COMPS)]
        square = cells[0] * cells[0]
        for c in range(1, COMPS):
            square = square + cells[c] * cells[c]
        coef = (2.0 - 4.0 * qua) + (4.0 * qua) * square
        for c in range(COMPS):
            q = cells[c]
            own = packed(lambda o: here[0](c, o))
            right = pltpu.roll(jnp.where(slot == 8, own, q), LANES - 1, 1)
            left = pltpu.roll(jnp.where(slot == 7, own, q), 1, 1)
            above = pltpu.roll(q, 7, 0)
            below = pltpu.roll(q, 1, 0)
            z_up = jnp.where(last_row, pltpu.roll(above, LANES - 16, 1), above)
            z_down = jnp.where(first_row, pltpu.roll(below, 16, 1), below)
            nsum = (down[1](c) + up[1](c)) + (left + right) + (z_up + z_down)
            new = mom[1](c) + dt * ((2.0 * kap) * nsum - coef * q)
            results.append((new, q + STEP * new))

    def store():
        for job, (*_, put) in enumerate(jobs):
            for c in range(COMPS):
                put(c, *results[job * COMPS + c])

    return store


def ingest_kernel(flags, field, momenta, *refs):
    mains, messages, (held, sems) = ((refs[:4], refs[4:8]), refs[8:10], refs[10:])
    copies = {
        (k, c): pltpu.make_async_copy(src.at[c], held.at[k, c], sems.at[k, c])
        for c in range(COMPS)
        for k, src in enumerate((field, momenta))
    }
    for copy in copies.values():
        copy.start()
    low = lanes() % 16 < 8
    odd = flags[1] == 1
    mirrored = jnp.broadcast_to(flags[0, :1, :], (NZ, LANES)) == 1
    for c in range(COMPS):
        copies[0, c].wait()
        copies[1, c].wait()
        lines = [[held[k, c, pl.ds(x, NZ, stride=WIDE), :] for x in range(WIDE)] for k in range(2)]
        for u in range(WIDE):
            packs = []
            for k in range(2):
                value = jnp.where(mirrored, lines[k][WIDE - 1 - u], lines[k][u])
                mains[k][u][c] = value
                packs.append(packed(lambda o: value[8 * o : 8 * o + 8, :]))
            right = jnp.where(low, packs[0], pltpu.roll(packs[1], 8, 1))
            left = jnp.where(low, pltpu.roll(packs[0], LANES - 8, 1), packs[1])
            messages[0][u, c] = jnp.where(odd, left, right)
            messages[1][u, c] = jnp.where(odd, right, left)


def ghost_kernel(flags, first, second, m1, k0, qg, pg, near, far):
    low = lanes() % 16 < 8
    odd = flags[1] == 1
    for u in range(WIDE):
        for c in range(COMPS):
            left = jnp.where(odd, first[u, c], second[u, c])
            right = jnp.where(odd, second[u, c], first[u, c])
            q = jnp.where(low, left, pltpu.roll(right, 8, 1))
            p = jnp.where(low, pltpu.roll(left, LANES - 8, 1), right)
            qg[u, c] = q
            pg[u, c] = p
            if u == WIDE - 1:
                near[c] = q
    write_main(far, 0, lambda c, o: m1[c, 8 * o : 8 * o + 8, :])
    write_main(far, SITES, lambda c, o: k0[c, 8 * o : 8 * o + 8, :])
    write_edge(far, 2 * SITES, lambda c: qg[0, c])
    write_edge(far, 2 * SITES + 16, lambda c: qg[1, c])
    write_edge(far, 2 * SITES + 32, lambda c: pg[0, c])


def fresh():
    return jnp.zeros((8, LANES), jnp.float32)


def step(around, moms, outs, par, dt, energy=None, edges=True):
    spans = [around[i : i + 3] for i in range(len(moms))]
    store = None
    if edges:
        jobs = [(*span, mom, store_edge(*out)) for span, mom, out in zip(spans, moms, outs)]
        store = edge_eval(jobs, par, dt)
    for span, mom, out in zip(spans, moms, outs):
        main_eval(*span, mom, store_main(*out), par, dt, energy)
    if edges:
        store()


def inside(ref, main, edge):
    def ghosts(c):
        value = ref[edge + 8 * (c % 2) : edge + 8 * (c % 2) + 8, :]
        return value if c < 2 else pltpu.roll(value, LANES - 8, 1)

    return (lambda c, o: ref[main + NZ * c + 8 * o : main + NZ * c + 8 * o + 8, :], ghosts)


def write_main(ref, main, load):
    for c in range(COMPS):
        for o in range(OCT):
            ref[main + NZ * c + 8 * o : main + NZ * c + 8 * o + 8, :] = load(c, o)


def write_edge(ref, edge, load):
    slot = lanes() % 16
    for c in range(2):
        both = jnp.where((slot >= 4) & (slot < 12), load(c), pltpu.roll(load(c + 2), 8, 1))
        ref[edge + 8 * c : edge + 8 * c + 8, :] = both


def inner_start(
    par, far, m0, m1, m2, m3, k0, k1, k2, k3, qg, pg, near, near_g, z, zp, q1, p1, q2, p2, q3, p3, energy, msg, msg_near
):
    par = settings(par)
    around = [layer_of(main, qg.at[u]) for u, main in enumerate((m0, m1, m2, m3))] + [layer_of(near, near_g)]
    total = [fresh(), False]
    held = [layer_of(mom, pg.at[u + 1]) for u, mom in enumerate((k1, k2, k3))]
    step(around, held, [(q1, p1), (q2, p2), (q3, p3)], par, 0.5 * STEP, total)
    write_main(msg, 0, joint(q1)[0])
    write_edge(msg, SITES, joint(q1)[1])
    write_main(msg_near, 0, joint(q3)[0])
    write_edge(msg_near, SITES, joint(q3)[1])
    store = store_main(z, zp)
    main_eval(layer_of(far), around[0], around[1], layer_of(k0), store, par, 0.5 * STEP, total)
    energy[...] = total[0]


def outer_first(par, beyond, far, m0, qg, pg, z, zp, q1, p1, q2, zg, n1, r1, hq, hp, nz, nzp, zpg):
    par = settings(par)
    outer, halo = (inside(beyond, 0, 2 * SITES + 16), inside(beyond, 0, 2 * SITES))
    halo = (layer_of(far)[0], halo[1])
    here = layer_of(m0, qg.at[0])

    def put(c, new_p, new_q):
        zpg[c] = new_p
        zg[c] = new_q

    edge_eval([(halo, here, (None, lambda c: qg[1, c]), (None, lambda c: pg[0, c]), put)], par, 0.5 * STEP)()
    step([outer, halo, here], [inside(beyond, SITES, 2 * SITES + 32)], [(hq, hp)], par, 0.5 * STEP)
    step([layer_of(z, zg), joint(q1), joint(q2)], [joint(p1)], [(n1, r1)], par, STEP)
    step([joint(hq), layer_of(z, zg), joint(q1)], [layer_of(zp, zpg)], [(nz, nzp)], par, STEP)


def inner_second(par, z, q1, p1, q2, p2, q3, p3, near, n1, r1, n2, r2, n3, r3, msg, msg_near):
    around = [joint(z), joint(q1), joint(q2), joint(q3), inside(near, 0, SITES)]
    moms = [joint(p1), joint(p2), joint(p3)]
    step(around, moms, [(n1, r1), (n2, r2), (n3, r3)], settings(par), STEP)
    write_main(msg, 0, joint(q1)[0])
    write_edge(msg, SITES, joint(q1)[1])
    write_main(msg, SITES + 16, joint(n1)[0])
    write_main(msg_near, 0, joint(n3)[0])
    write_edge(msg_near, SITES, joint(n3)[1])


def outer_kernel(par, beyond, hq, hp, zold, zold_g, z, zp, old1, q1, p1, q2, nhq, nhp, nz, nzp, n1, r1):
    par = settings(par)
    step([inside(beyond, 0, SITES), joint(hq), layer_of(zold, zold_g)], [joint(hp)], [(nhq, nhp)], par, STEP)
    step([joint(nhq), joint(z), joint(old1)], [joint(zp)], [(nz, nzp)], par, STEP)
    step([joint(nz), joint(q1), joint(q2)], [joint(p1)], [(n1, r1)], par, STEP)


def inner_kernel(par, q1, q2, p2, q3, p3, near, n2, r2, n3, r3, msg):
    around = [joint(q1), joint(q2), joint(q3), inside(near, 0, SITES)]
    step(around, [joint(p2), joint(p3)], [(n2, r2), (n3, r3)], settings(par), STEP)
    write_main(msg, 0, joint(n3)[0])
    write_edge(msg, SITES, joint(n3)[1])


def inner_third(par, q1, q2, p2, q3, p3, near, n2, r2, n3, r3, msg, whole):
    around = [joint(q1), joint(q2), joint(q3), inside(near, 0, SITES)]
    step(around, [joint(p2), joint(p3)], [(n2, r2), (n3, r3)], settings(par), STEP)
    write_main(msg, 0, joint(n3)[0])
    for u, ref in enumerate((n2, n3)):
        for c in range(COMPS):
            whole[u, c] = ref[c, :NZ, :]


def inner_final(par, q1, q2, p2, q3, p3, near, r2, r3, energy):
    around = [joint(q1), joint(q2), joint(q3), inside(near, 0, 0)]
    total = [fresh(), True]
    outs = [(None, r2), (None, r3)]
    step(around, [joint(p2), joint(p3)], outs, settings(par), 0.5 * STEP, total, False)
    energy[...] = total[0]


def outer_last(
    par, beyond, hq, hp, zold, z, zp, old1, q1, p1, q2, r2, r3, start, more,
    whole, energy, nhq, nhp, nz, nzp, last,
):
    par = settings(par)
    step([inside(beyond, 0, SITES), joint(hq), joint(zold)], [joint(hp)], [(nhq, nhp)], par, STEP)
    step([joint(nhq), joint(z), joint(old1)], [joint(zp)], [(nz, nzp)], par, STEP)
    store = store_main(last, None)
    outer = inside(beyond, SITES + 16, 0)
    main_eval(outer, joint(nhq), joint(z), joint(nhp), store, par, STEP, None)
    total = [more[...], True]
    store = store_main(None, whole.at[2])
    main_eval(layer_of(last), joint(nz), joint(q1), joint(nzp), store, par, 0.5 * STEP, total)
    store = store_main(None, whole.at[3])
    main_eval(joint(nz), joint(q1), joint(q2), joint(p1), store, par, 0.5 * STEP, total)
    before = jnp.sum(start[...], axis=0, keepdims=True)
    after = jnp.sum(total[0], axis=0, keepdims=True)
    row = rows()
    energy[...] = jnp.where(row == 0, before, jnp.where(row == 1, after, 0.0))
    for c in range(COMPS):
        whole[0, c] = nz[c, :NZ, :]
        whole[1, c] = q1[c, :NZ, :]
        whole[4, c] = r2[c]
        whole[5, c] = r3[c]


def pack_kernel(late, out):
    out[...] = late[...]


def pick_kernel(acceptance, flags, choice):
    position = flags[2]
    partner = position
    for replica in range(acceptance.shape[0]):
        partner = jnp.where(position == replica, acceptance[replica], partner)
    beside = position ^ 1
    choice[0] = flags[0]
    choice[1] = (partner == beside).astype(jnp.int32)
    choice[2] = ((partner != beside) & (partner != position)).astype(jnp.int32)


def place_kernel(choice, *refs):
    late, early, (new_q, new_p, held, sems) = (refs[:3], refs[3:6], refs[6:])
    mirrored, first, second = (jnp.broadcast_to(choice[i, :1, :], (NZ, LANES)) == 1 for i in range(3))

    def picked(sources, u, c):
        return jnp.where(first, sources[1][u, c], jnp.where(second, sources[2][u, c], sources[0][u, c]))

    copies = []
    for k, out in enumerate((new_q, new_p)):
        for c in range(COMPS):
            if k == 1:
                layers = [picked(late, u + 2, c) for u in range(WIDE)]
            else:
                layers = [picked(late, u, c) if u < 2 else picked(early, u - 2, c) for u in range(WIDE)]
            for x in range(WIDE):
                value = jnp.where(mirrored, layers[WIDE - 1 - x], layers[x])
                held[k, c, pl.ds(x, NZ, stride=WIDE), :] = value
            copies.append(pltpu.make_async_copy(held.at[k, c], out.at[c], sems.at[k, c]))
            copies[-1].start()
    for copy in copies:
        copy.wait()


def total_kernel(volume, *refs):
    *parts, out = refs
    total = sum((ref[...] for ref in parts[1:]), parts[0][...])
    start, finish = (jnp.sum(total[i : i + 1, :], axis=1, keepdims=True) for i in range(2))
    lane = lax.broadcasted_iota(jnp.int32, (1, 2), 1)
    out[...] = jnp.where(lane == 0, start, finish) * (1.0 / volume)


def run(kernel, outs, arrays, scratch=(), raw=(), after=(), held=True, scalars=()):
    vmem, hbm = (pl.BlockSpec(memory_space=pltpu.VMEM), pl.BlockSpec(memory_space=pltpu.HBM))
    given = len(scalars) + len(arrays) + len(raw)

    def body(*refs):
        kernel(*refs[:given], *refs[given + len(after) :])

    space = pltpu.VMEM if held else pltpu.HBM
    return pl.pallas_call(
        body,
        out_shape=[space(out.shape, out.dtype) for out in outs],
        in_specs=[pl.BlockSpec(memory_space=pltpu.SMEM)] * len(scalars)
        + [vmem] * len(arrays) + [hbm] * len(raw) + [pl.BlockSpec(memory_space=pl.ANY)] * len(after),
        out_specs=[vmem if held else hbm] * len(outs),
        scratch_shapes=list(scratch),
        cost_estimate=pl.CostEstimate(flops=4000, bytes_accessed=1000, transcendentals=0),
        compiler_params=pltpu.CompilerParams(vmem_limit_bytes=12 * 1024 * 1024),
    )(
        *scalars,
        *(pltpu.with_memory_space_constraint(value, pltpu.VMEM) for value in arrays),
        *(pltpu.with_memory_space_constraint(value, pltpu.HBM) for value in raw),
        *after,
    )


def pair_swap(value, axis, other):
    return lax.ppermute(value, axis, [(i, other(i)) for i in range(lax.axis_size(axis)) if other(i) is not None])


def local(field, momenta, kappa, quartic, acceptance):
    gx, gy, reps = (lax.axis_size("gx"), lax.axis_size("gy"), lax.axis_size("rep"))
    volume = NZ * WIDE * LANES * gx * gy
    core = lax.axis_index("gx") % 2
    places = [core, lax.axis_index("gy") % 2, lax.axis_index("rep")]
    flags = jnp.broadcast_to(jnp.stack(places)[:, None, None], (3, 8, LANES)).astype(jnp.int32)
    par = jnp.broadcast_to(jnp.concatenate([kappa, quartic])[:, None, None], (2, 8, LANES))
    (choice,) = run(pick_kernel, [jax.ShapeDtypeStruct((3, 8, LANES), jnp.int32)], [flags], scalars=[acceptance])

    def far(value):
        return pair_swap(value, "gx", lambda i: (i + 1) % gx if i % 2 == 1 else (i - 1) % gx)

    def near(value):
        return pair_swap(value, "gx", lambda i: i ^ 1)

    def beside(value, parity):
        return pair_swap(value, "gy", lambda i: (i + 1) % gy if i % 2 == parity else (i - 1) % gy)

    def exchanged(value):
        first = pair_swap(value, "rep", lambda i: i ^ 1 if i ^ 1 < reps else None)
        second = pair_swap(value, "rep", lambda i: ((i - 1) ^ 1) + 1 if 0 < i and ((i - 1) ^ 1) + 1 < reps else None)
        return (first, second)

    main, both = (f32(COMPS, NZ, LANES), f32(COMPS, NZ + 8, LANES))
    edges, whole, vreg = (f32(WIDE, COMPS, 8, LANES), f32(WIDE, COMPS, NZ, LANES), f32(8, LANES))
    edge, side = (f32(COMPS, 8, LANES), f32(SITES + 16, LANES))

    m0, m1, m2, m3, k0, k1, k2, k3, to_first, to_second = run(
        ingest_kernel,
        [main] * 8 + [edges] * 2,
        [flags],
        scratch=[pltpu.VMEM((2, COMPS, NZ * WIDE, LANES), jnp.float32), pltpu.SemaphoreType.DMA((2, COMPS))],
        raw=[value.reshape(COMPS, NZ * WIDE, LANES) for value in (field, momenta)],
    )
    far0, near0 = (far(m0), near(m3))
    first, second = (beside(to_first, 0), beside(to_second, 1))
    qg, pg, near_g, to_far = run(
        ghost_kernel, [edges, edges, edge, f32(2 * SITES + 48, LANES)], [flags, first, second, m1, k0]
    )
    near_ghost, beyond0 = (near(near_g), far(to_far))
    z1, zp1, a1, b1, a2, b2, a3, b3, start, msg, to_near = run(
        inner_start,
        [main, main] + [both] * 6 + [vreg, f32(SITES + 24, LANES), side],
        [par, far0, m0, m1, m2, m3, k0, k1, k2, k3, qg, pg, near0, near_ghost],
    )
    beyond1, near1 = (far(msg), near(to_near))
    arrays = [par, a1, a2, b2, a3, b3, near1]
    c2, d2, c3, d3, to_near = run(inner_kernel, [both] * 4 + [side], arrays, after=[choice])
    near2 = near(to_near)
    zg1, c1, d1, hq1, hp1, z2, zp2 = run(
        outer_first,
        [edge] + [both] * 6,
        [par, beyond0, far0, m0, qg, pg, z1, zp1, a1, b1, a2],
        scratch=[pltpu.VMEM((COMPS, 8, LANES), jnp.float32)],
    )
    e1, f1, e2, f2, e3, f3, msg, to_near = run(
        inner_second,
        [both] * 6 + [f32(2 * SITES + 16, LANES), side],
        [par, z2, c1, d1, c2, d2, c3, d3, near2],
    )
    beyond2 = far(msg)
    near3 = near(to_near)
    hq2, hp2, z3, zp3, g1, h1 = run(
        outer_kernel,
        [both] * 6,
        [par, beyond1, hq1, hp1, z1, zg1, z2, zp2, c1, e1, f1, e2],
    )
    g2, h2, g3, h3, to_near, early = run(
        inner_third,
        [both] * 4 + [f32(SITES, LANES), f32(2, COMPS, NZ, LANES)],
        [par, e1, e2, f2, e3, f3, near3],
        after=[beyond1],
    )
    near4 = near(to_near)
    first_early, second_early = exchanged(early)
    r2, r3, more = run(inner_final, [main, main, vreg], [par, g1, g2, h2, g3, h3, near4])
    late, energy = run(
        outer_last,
        [f32(6, COMPS, NZ, LANES), vreg],
        [par, beyond2, hq2, hp2, z2, z3, zp3, e1, g1, h1, g2, r2, r3, start, more],
        scratch=[pltpu.VMEM((COMPS, NZ + 8, LANES), jnp.float32)] * 4 + [pltpu.VMEM((COMPS, NZ, LANES), jnp.float32)],
    )
    (late,) = run(pack_kernel, [f32(6, COMPS, NZ, LANES)], [late], after=[first_early, second_early])
    first_late, second_late = exchanged(late)

    new_q, new_p = run(
        place_kernel,
        [f32(COMPS, NZ * WIDE, LANES)] * 2,
        [choice, late, first_late, second_late, early, first_early, second_early],
        scratch=[pltpu.VMEM((2, COMPS, NZ * WIDE, LANES), jnp.float32), pltpu.SemaphoreType.DMA((2, COMPS))],
        held=False,
    )
    energy = energy + near(energy)
    moved = [pair_swap(energy, "gx", lambda i, k=k: i ^ (4 * k)) for k in range(1, gx // 4)]
    energy = sum(moved, energy)
    for bit in (1, 2):
        energy = energy + pair_swap(energy, "gy", lambda i, bit=bit: i ^ bit)

    def across(i_bit, j_bit):
        pairs = [(i * gy + j, (i ^ i_bit) * gy + (j ^ j_bit)) for i in range(gx) for j in range(gy)]
        return lax.ppermute(energy, ("gx", "gy"), pairs)

    parts = [energy, across(2, 3)]
    placed_first = [pltpu.with_memory_space_constraint(value, pltpu.HBM) for value in (new_q, new_p)]
    (energy,) = run(functools.partial(total_kernel, volume), [f32(1, 2)], parts, after=placed_first)
    return (new_q.reshape(field.shape), new_p.reshape(field.shape), energy)


def solution(mesh):
    placed = (
        P("rep", None, None, "gx", "gy"),
        P("rep", None, None, "gx", "gy"),
        P("rep"),
        P("rep"),
        P(),
    )
    return jax.shard_map(
        local,
        mesh=mesh,
        in_specs=placed,
        out_specs=(
            P("rep", None, None, "gx", "gy"),
            P("rep", None, None, "gx", "gy"),
            P("rep", None),
        ),
        check_vma=False,
    )
```

```python
import functools

import jax
import jax.numpy as jnp
from jax import lax
from jax.experimental import pallas as pl
from jax.experimental.pallas import tpu as pltpu
from jax.sharding import PartitionSpec as P

LEAPS = 4
STEP = 0.05
COMPS = 4
NZ = 64
OCT = NZ // 8
WIDE = 4
LANES = 128
SITES = COMPS * NZ


def f32(*shape):
    return jax.ShapeDtypeStruct(shape, jnp.float32)


def lanes():
    return lax.broadcasted_iota(jnp.int32, (8, LANES), 1)


def rows():
    return lax.broadcasted_iota(jnp.int32, (8, LANES), 0)


def packed(load):
    octet = lanes() // 16
    out = None
    for o in range(OCT):
        moved = pltpu.roll(load(o), (16 * o + 8) % LANES, 1)
        out = moved if out is None else jnp.where(octet == o, moved, out)
    return out


def layer_of(main, edge=None):
    return (lambda c, o: main[c, 8 * o : 8 * o + 8, :], None if edge is None else (lambda c: edge[c]))


def joint(ref):
    return (lambda c, o: ref[c, 8 * o : 8 * o + 8, :], lambda c: ref[c, NZ : NZ + 8, :])


def store_main(q, p):
    def put(c, o, new_p, new_q):
        if p is not None:
            p[c, 8 * o : 8 * o + 8, :] = new_p
        if q is not None:
            q[c, 8 * o : 8 * o + 8, :] = new_q

    return put


def store_edge(q, p):
    def put(c, new_p, new_q):
        p[c, NZ : NZ + 8, :] = new_p
        q[c, NZ : NZ + 8, :] = new_q

    return put


def settings(ref):
    row = lax.broadcasted_iota(jnp.int32, (LANES, LANES), 0)
    lane = lax.broadcasted_iota(jnp.int32, (LANES, LANES), 1)
    mix = jnp.where(jnp.abs(row - lane) == 1, 1.0, 0.0).astype(jnp.bfloat16)
    return (ref[0], ref[1], jnp.concatenate([mix, mix], axis=0))


def main_eval(down, here, up, mom, put, par, dt, energy):
    kap, qua, mix = par
    lane, row = (lanes(), rows())
    zero_lane, last_lane = (lane == 0, lane == LANES - 1)
    first_row, last_row = (row == 0, row == 7)
    nsums = {}
    for c in range(COMPS):
        cells = [here[0](c, o) for o in range(OCT)]
        edge = here[1](c)
        whole = jnp.concatenate(cells, axis=0)
        high = whole.astype(jnp.bfloat16)
        low = (whole - high.astype(jnp.float32)).astype(jnp.bfloat16)
        beside = jnp.dot(jnp.concatenate([high, low], axis=1), mix, preferred_element_type=jnp.float32)
        left = [pltpu.roll(edge, (121 - 16 * o) % LANES, 1) for o in range(OCT)]
        right = [pltpu.roll(edge, (119 - 16 * o) % LANES, 1) for o in range(OCT)]
        above = [pltpu.roll(q, 7, 0) for q in cells]
        below = [pltpu.roll(q, 1, 0) for q in cells]
        for o in range(OCT):
            z_up = jnp.where(last_row, above[(o + 1) % OCT], above[o])
            z_down = jnp.where(first_row, below[o - 1], below[o])
            ghost = jnp.where(zero_lane, left[o], jnp.where(last_lane, right[o], 0.0))
            y_sum = beside[8 * o : 8 * o + 8] + ghost
            nsums[c, o] = (down[0](c, o) + up[0](c, o)) + y_sum + (z_up + z_down)
    waiting = []
    for o in range(OCT):
        cells = [here[0](c, o) for c in range(COMPS)]
        moms = [mom[0](c, o) for c in range(COMPS)]
        square = cells[0] * cells[0]
        for c in range(1, COMPS):
            square = square + cells[c] * cells[c]
        coef = (2.0 - 4.0 * qua) + (4.0 * qua) * square
        dots = None
        results = []
        for c in range(COMPS):
            q, p, nsum = (cells[c], moms[c], nsums[c, o])
            new = p + dt * ((2.0 * kap) * nsum - coef * q)
            results.append((new, q + STEP * new))
            if energy is not None:
                dots = q * nsum if dots is None else dots + q * nsum
                kin = new if energy[1] else p
                energy[0] = energy[0] + 0.5 * (kin * kin)
        if energy is not None:
            energy[0] = energy[0] + (square - kap * dots + qua * ((square - 1.0) * (square - 1.0)))
        waiting.append((o, results))
        while len(waiting) > (2 if o < OCT - 1 else 0):
            at, ready = waiting.pop(0)
            for c in range(COMPS):
                put(c, at, *ready[c])


def edge_eval(jobs, par, dt):
    kap, qua, _ = par
    lane, row = (lanes(), rows())
    slot = lane % 16
    first_row, last_row = (row == 0, row == 7)
    results = []
    for down, here, up, mom, _ in jobs:
        cells = [here[1](c) for c in range(COMPS)]
        square = cells[0] * cells[0]
        for c in range(1, COMPS):
            square = square + cells[c] * cells[c]
        coef = (2.0 - 4.0 * qua) + (4.0 * qua) * square
        for c in range(COMPS):
            q = cells[c]
            own = packed(lambda o: here[0](c, o))
            right = pltpu.roll(jnp.where(slot == 8, own, q), LANES - 1, 1)
            left = pltpu.roll(jnp.where(slot == 7, own, q), 1, 1)
            above = pltpu.roll(q, 7, 0)
            below = pltpu.roll(q, 1, 0)
            z_up = jnp.where(last_row, pltpu.roll(above, LANES - 16, 1), above)
            z_down = jnp.where(first_row, pltpu.roll(below, 16, 1), below)
            nsum = (down[1](c) + up[1](c)) + (left + right) + (z_up + z_down)
            new = mom[1](c) + dt * ((2.0 * kap) * nsum - coef * q)
            results.append((new, q + STEP * new))

    def store():
        for job, (*_, put) in enumerate(jobs):
            for c in range(COMPS):
                put(c, *results[job * COMPS + c])

    return store


def ingest_kernel(flags, field, momenta, *refs):
    mains, messages, (held, sems) = ((refs[:4], refs[4:8]), refs[8:10], refs[10:])
    copies = {
        (k, c): pltpu.make_async_copy(src.at[c], held.at[k, c], sems.at[k, c])
        for c in range(COMPS)
        for k, src in enumerate((field, momenta))
    }
    for copy in copies.values():
        copy.start()
    low = lanes() % 16 < 8
    odd = flags[1] == 1
    mirrored = jnp.broadcast_to(flags[0, :1, :], (NZ, LANES)) == 1
    for c in range(COMPS):
        copies[0, c].wait()
        copies[1, c].wait()
        lines = [[held[k, c, pl.ds(x, NZ, stride=WIDE), :] for x in range(WIDE)] for k in range(2)]
        for u in range(WIDE):
            packs = []
            for k in range(2):
                value = jnp.where(mirrored, lines[k][WIDE - 1 - u], lines[k][u])
                mains[k][u][c] = value
                packs.append(packed(lambda o: value[8 * o : 8 * o + 8, :]))
            right = jnp.where(low, packs[0], pltpu.roll(packs[1], 8, 1))
            left = jnp.where(low, pltpu.roll(packs[0], LANES - 8, 1), packs[1])
            messages[0][u, c] = jnp.where(odd, left, right)
            messages[1][u, c] = jnp.where(odd, right, left)


def ghost_kernel(flags, first, second, m1, k0, qg, pg, near, far):
    low = lanes() % 16 < 8
    odd = flags[1] == 1
    for u in range(WIDE):
        for c in range(COMPS):
            left = jnp.where(odd, first[u, c], second[u, c])
            right = jnp.where(odd, second[u, c], first[u, c])
            q = jnp.where(low, left, pltpu.roll(right, 8, 1))
            p = jnp.where(low, pltpu.roll(left, LANES - 8, 1), right)
            qg[u, c] = q
            pg[u, c] = p
            if u == WIDE - 1:
                near[c] = q
    write_main(far, 0, lambda c, o: m1[c, 8 * o : 8 * o + 8, :])
    write_main(far, SITES, lambda c, o: k0[c, 8 * o : 8 * o + 8, :])
    write_edge(far, 2 * SITES, lambda c: qg[0, c])
    write_edge(far, 2 * SITES + 16, lambda c: qg[1, c])
    write_edge(far, 2 * SITES + 32, lambda c: pg[0, c])


def fresh():
    return jnp.zeros((8, LANES), jnp.float32)


def step(around, moms, outs, par, dt, energy=None, edges=True):
    spans = [around[i : i + 3] for i in range(len(moms))]
    store = None
    if edges:
        jobs = [(*span, mom, store_edge(*out)) for span, mom, out in zip(spans, moms, outs)]
        store = edge_eval(jobs, par, dt)
    for span, mom, out in zip(spans, moms, outs):
        main_eval(*span, mom, store_main(*out), par, dt, energy)
    if edges:
        store()


def inside(ref, main, edge):
    def ghosts(c):
        value = ref[edge + 8 * (c % 2) : edge + 8 * (c % 2) + 8, :]
        return value if c < 2 else pltpu.roll(value, LANES - 8, 1)

    return (lambda c, o: ref[main + NZ * c + 8 * o : main + NZ * c + 8 * o + 8, :], ghosts)


def write_main(ref, main, load):
    for c in range(COMPS):
        for o in range(OCT):
            ref[main + NZ * c + 8 * o : main + NZ * c + 8 * o + 8, :] = load(c, o)


def write_edge(ref, edge, load):
    slot = lanes() % 16
    for c in range(2):
        both = jnp.where((slot >= 4) & (slot < 12), load(c), pltpu.roll(load(c + 2), 8, 1))
        ref[edge + 8 * c : edge + 8 * c + 8, :] = both


def inner_start(
    par, far, m0, m1, m2, m3, k0, k1, k2, k3, qg, pg, near, near_g, z, zp, q1, p1, q2, p2, q3, p3, energy, msg, msg_near
):
    par = settings(par)
    around = [layer_of(main, qg.at[u]) for u, main in enumerate((m0, m1, m2, m3))] + [layer_of(near, near_g)]
    total = [fresh(), False]
    held = [layer_of(mom, pg.at[u + 1]) for u, mom in enumerate((k1, k2, k3))]
    step(around, held, [(q1, p1), (q2, p2), (q3, p3)], par, 0.5 * STEP, total)
    write_main(msg, 0, joint(q1)[0])
    write_edge(msg, SITES, joint(q1)[1])
    write_main(msg_near, 0, joint(q3)[0])
    write_edge(msg_near, SITES, joint(q3)[1])
    store = store_main(z, zp)
    main_eval(layer_of(far), around[0], around[1], layer_of(k0), store, par, 0.5 * STEP, total)
    energy[...] = total[0]


def outer_first(par, beyond, far, m0, qg, pg, z, zp, q1, p1, q2, zg, n1, r1, hq, hp, nz, nzp, zpg):
    par = settings(par)
    outer, halo = (inside(beyond, 0, 2 * SITES + 16), inside(beyond, 0, 2 * SITES))
    halo = (layer_of(far)[0], halo[1])
    here = layer_of(m0, qg.at[0])

    def put(c, new_p, new_q):
        zpg[c] = new_p
        zg[c] = new_q

    edge_eval([(halo, here, (None, lambda c: qg[1, c]), (None, lambda c: pg[0, c]), put)], par, 0.5 * STEP)()
    step([outer, halo, here], [inside(beyond, SITES, 2 * SITES + 32)], [(hq, hp)], par, 0.5 * STEP)
    step([layer_of(z, zg), joint(q1), joint(q2)], [joint(p1)], [(n1, r1)], par, STEP)
    step([joint(hq), layer_of(z, zg), joint(q1)], [layer_of(zp, zpg)], [(nz, nzp)], par, STEP)


def inner_second(par, z, q1, p1, q2, p2, q3, p3, near, n1, r1, n2, r2, n3, r3, msg, msg_near):
    around = [joint(z), joint(q1), joint(q2), joint(q3), inside(near, 0, SITES)]
    moms = [joint(p1), joint(p2), joint(p3)]
    step(around, moms, [(n1, r1), (n2, r2), (n3, r3)], settings(par), STEP)
    write_main(msg, 0, joint(q1)[0])
    write_edge(msg, SITES, joint(q1)[1])
    write_main(msg, SITES + 16, joint(n1)[0])
    write_main(msg_near, 0, joint(n3)[0])
    write_edge(msg_near, SITES, joint(n3)[1])


def outer_kernel(par, beyond, hq, hp, zold, zold_g, z, zp, old1, q1, p1, q2, nhq, nhp, nz, nzp, n1, r1):
    par = settings(par)
    step([inside(beyond, 0, SITES), joint(hq), layer_of(zold, zold_g)], [joint(hp)], [(nhq, nhp)], par, STEP)
    step([joint(nhq), joint(z), joint(old1)], [joint(zp)], [(nz, nzp)], par, STEP)
    step([joint(nz), joint(q1), joint(q2)], [joint(p1)], [(n1, r1)], par, STEP)


def inner_kernel(par, q1, q2, p2, q3, p3, near, n2, r2, n3, r3, msg):
    around = [joint(q1), joint(q2), joint(q3), inside(near, 0, SITES)]
    step(around, [joint(p2), joint(p3)], [(n2, r2), (n3, r3)], settings(par), STEP)
    write_main(msg, 0, joint(n3)[0])
    write_edge(msg, SITES, joint(n3)[1])


def inner_third(par, q1, q2, p2, q3, p3, near, n2, r2, n3, r3, msg, whole):
    around = [joint(q1), joint(q2), joint(q3), inside(near, 0, SITES)]
    step(around, [joint(p2), joint(p3)], [(n2, r2), (n3, r3)], settings(par), STEP)
    write_main(msg, 0, joint(n3)[0])
    for u, ref in enumerate((n2, n3)):
        for c in range(COMPS):
            whole[u, c] = ref[c, :NZ, :]


def inner_final(par, q1, q2, p2, q3, p3, near, r2, r3, energy):
    around = [joint(q1), joint(q2), joint(q3), inside(near, 0, 0)]
    total = [fresh(), True]
    outs = [(None, r2), (None, r3)]
    step(around, [joint(p2), joint(p3)], outs, settings(par), 0.5 * STEP, total, False)
    energy[...] = total[0]


def outer_last(
    par, beyond, hq, hp, zold, z, zp, old1, q1, p1, q2, r2, r3, start, more,
    whole, energy, nhq, nhp, nz, nzp, last,
):
    par = settings(par)
    step([inside(beyond, 0, SITES), joint(hq), joint(zold)], [joint(hp)], [(nhq, nhp)], par, STEP)
    step([joint(nhq), joint(z), joint(old1)], [joint(zp)], [(nz, nzp)], par, STEP)
    store = store_main(last, None)
    outer = inside(beyond, SITES + 16, 0)
    main_eval(outer, joint(nhq), joint(z), joint(nhp), store, par, STEP, None)
    total = [more[...], True]
    store = store_main(None, whole.at[2])
    main_eval(layer_of(last), joint(nz), joint(q1), joint(nzp), store, par, 0.5 * STEP, total)
    store = store_main(None, whole.at[3])
    main_eval(joint(nz), joint(q1), joint(q2), joint(p1), store, par, 0.5 * STEP, total)
    before = jnp.sum(start[...], axis=0, keepdims=True)
    after = jnp.sum(total[0], axis=0, keepdims=True)
    row = rows()
    energy[...] = jnp.where(row == 0, before, jnp.where(row == 1, after, 0.0))
    for c in range(COMPS):
        whole[0, c] = nz[c, :NZ, :]
        whole[1, c] = q1[c, :NZ, :]
        whole[4, c] = r2[c]
        whole[5, c] = r3[c]


def pack_kernel(late, out):
    out[...] = late[...]


def pick_kernel(acceptance, flags, choice):
    position = flags[2]
    partner = position
    for replica in range(acceptance.shape[0]):
        partner = jnp.where(position == replica, acceptance[replica], partner)
    beside = position ^ 1
    choice[0] = flags[0]
    choice[1] = (partner == beside).astype(jnp.int32)
    choice[2] = ((partner != beside) & (partner != position)).astype(jnp.int32)


def place_kernel(choice, *refs):
    late, early, (new_q, new_p, held, sems) = (refs[:3], refs[3:6], refs[6:])
    mirrored, first, second = (jnp.broadcast_to(choice[i, :1, :], (NZ, LANES)) == 1 for i in range(3))

    def picked(sources, u, c):
        return jnp.where(first, sources[1][u, c], jnp.where(second, sources[2][u, c], sources[0][u, c]))

    copies = []
    for k, out in enumerate((new_q, new_p)):
        for c in range(COMPS):
            if k == 1:
                layers = [picked(late, u + 2, c) for u in range(WIDE)]
            else:
                layers = [picked(late, u, c) if u < 2 else picked(early, u - 2, c) for u in range(WIDE)]
            for x in range(WIDE):
                value = jnp.where(mirrored, layers[WIDE - 1 - x], layers[x])
                held[k, c, pl.ds(x, NZ, stride=WIDE), :] = value
            copies.append(pltpu.make_async_copy(held.at[k, c], out.at[c], sems.at[k, c]))
            copies[-1].start()
    for copy in copies:
        copy.wait()


def total_kernel(volume, *refs):
    *parts, out = refs
    total = sum((ref[...] for ref in parts[1:]), parts[0][...])
    start, finish = (jnp.sum(total[i : i + 1, :], axis=1, keepdims=True) for i in range(2))
    lane = lax.broadcasted_iota(jnp.int32, (1, 2), 1)
    out[...] = jnp.where(lane == 0, start, finish) * (1.0 / volume)


def run(kernel, outs, arrays, scratch=(), raw=(), after=(), held=True, scalars=()):
    vmem, hbm = (pl.BlockSpec(memory_space=pltpu.VMEM), pl.BlockSpec(memory_space=pltpu.HBM))
    given = len(scalars) + len(arrays) + len(raw)

    def body(*refs):
        kernel(*refs[:given], *refs[given + len(after) :])

    space = pltpu.VMEM if held else pltpu.HBM
    return pl.pallas_call(
        body,
        out_shape=[space(out.shape, out.dtype) for out in outs],
        in_specs=[pl.BlockSpec(memory_space=pltpu.SMEM)] * len(scalars)
        + [vmem] * len(arrays) + [hbm] * len(raw) + [pl.BlockSpec(memory_space=pl.ANY)] * len(after),
        out_specs=[vmem if held else hbm] * len(outs),
        scratch_shapes=list(scratch),
        cost_estimate=pl.CostEstimate(flops=4000, bytes_accessed=1000, transcendentals=0),
        compiler_params=pltpu.CompilerParams(vmem_limit_bytes=12 * 1024 * 1024),
    )(
        *scalars,
        *(pltpu.with_memory_space_constraint(value, pltpu.VMEM) for value in arrays),
        *(pltpu.with_memory_space_constraint(value, pltpu.HBM) for value in raw),
        *after,
    )


def pair_swap(value, axis, other):
    return lax.ppermute(value, axis, [(i, other(i)) for i in range(lax.axis_size(axis)) if other(i) is not None])


def local(field, momenta, kappa, quartic, acceptance):
    gx, gy, reps = (lax.axis_size("gx"), lax.axis_size("gy"), lax.axis_size("rep"))
    volume = NZ * WIDE * LANES * gx * gy
    core = lax.axis_index("gx") % 2
    places = [core, lax.axis_index("gy") % 2, lax.axis_index("rep")]
    flags = jnp.broadcast_to(jnp.stack(places)[:, None, None], (3, 8, LANES)).astype(jnp.int32)
    par = jnp.broadcast_to(jnp.concatenate([kappa, quartic])[:, None, None], (2, 8, LANES))
    (choice,) = run(pick_kernel, [jax.ShapeDtypeStruct((3, 8, LANES), jnp.int32)], [flags], scalars=[acceptance])

    def far(value):
        return pair_swap(value, "gx", lambda i: (i + 1) % gx if i % 2 == 1 else (i - 1) % gx)

    def near(value):
        return pair_swap(value, "gx", lambda i: i ^ 1)

    def beside(value, parity):
        return pair_swap(value, "gy", lambda i: (i + 1) % gy if i % 2 == parity else (i - 1) % gy)

    def exchanged(value):
        first = pair_swap(value, "rep", lambda i: i ^ 1 if i ^ 1 < reps else None)
        second = pair_swap(value, "rep", lambda i: ((i - 1) ^ 1) + 1 if 0 < i and ((i - 1) ^ 1) + 1 < reps else None)
        return (first, second)

    main, both = (f32(COMPS, NZ, LANES), f32(COMPS, NZ + 8, LANES))
    edges, whole, vreg = (f32(WIDE, COMPS, 8, LANES), f32(WIDE, COMPS, NZ, LANES), f32(8, LANES))
    edge, side = (f32(COMPS, 8, LANES), f32(SITES + 16, LANES))

    m0, m1, m2, m3, k0, k1, k2, k3, to_first, to_second = run(
        ingest_kernel,
        [main] * 8 + [edges] * 2,
        [flags],
        scratch=[pltpu.VMEM((2, COMPS, NZ * WIDE, LANES), jnp.float32), pltpu.SemaphoreType.DMA((2, COMPS))],
        raw=[value.reshape(COMPS, NZ * WIDE, LANES) for value in (field, momenta)],
    )
    far0, near0 = (far(m0), near(m3))
    first, second = (beside(to_first, 0), beside(to_second, 1))
    qg, pg, near_g, to_far = run(
        ghost_kernel, [edges, edges, edge, f32(2 * SITES + 48, LANES)], [flags, first, second, m1, k0]
    )
    near_ghost, beyond0 = (near(near_g), far(to_far))
    z1, zp1, a1, b1, a2, b2, a3, b3, start, msg, to_near = run(
        inner_start,
        [main, main] + [both] * 6 + [vreg, f32(SITES + 24, LANES), side],
        [par, far0, m0, m1, m2, m3, k0, k1, k2, k3, qg, pg, near0, near_ghost],
    )
    beyond1, near1 = (far(msg), near(to_near))
    arrays = [par, a1, a2, b2, a3, b3, near1]
    c2, d2, c3, d3, to_near = run(inner_kernel, [both] * 4 + [side], arrays, after=[choice])
    near2 = near(to_near)
    zg1, c1, d1, hq1, hp1, z2, zp2 = run(
        outer_first,
        [edge] + [both] * 6,
        [par, beyond0, far0, m0, qg, pg, z1, zp1, a1, b1, a2],
        scratch=[pltpu.VMEM((COMPS, 8, LANES), jnp.float32)],
    )
    e1, f1, e2, f2, e3, f3, msg, to_near = run(
        inner_second,
        [both] * 6 + [f32(2 * SITES + 16, LANES), side],
        [par, z2, c1, d1, c2, d2, c3, d3, near2],
    )
    beyond2 = far(msg)
    near3 = near(to_near)
    hq2, hp2, z3, zp3, g1, h1 = run(
        outer_kernel,
        [both] * 6,
        [par, beyond1, hq1, hp1, z1, zg1, z2, zp2, c1, e1, f1, e2],
    )
    g2, h2, g3, h3, to_near, early = run(
        inner_third,
        [both] * 4 + [f32(SITES, LANES), f32(2, COMPS, NZ, LANES)],
        [par, e1, e2, f2, e3, f3, near3],
        after=[beyond1],
    )
    near4 = near(to_near)
    first_early, second_early = exchanged(early)
    r2, r3, more = run(inner_final, [main, main, vreg], [par, g1, g2, h2, g3, h3, near4])
    late, energy = run(
        outer_last,
        [f32(6, COMPS, NZ, LANES), vreg],
        [par, beyond2, hq2, hp2, z2, z3, zp3, e1, g1, h1, g2, r2, r3, start, more],
        scratch=[pltpu.VMEM((COMPS, NZ + 8, LANES), jnp.float32)] * 4 + [pltpu.VMEM((COMPS, NZ, LANES), jnp.float32)],
    )
    (late,) = run(pack_kernel, [f32(6, COMPS, NZ, LANES)], [late], after=[first_early, second_early])
    first_late, second_late = exchanged(late)

    new_q, new_p = run(
        place_kernel,
        [f32(COMPS, NZ * WIDE, LANES)] * 2,
        [choice, late, first_late, second_late, early, first_early, second_early],
        scratch=[pltpu.VMEM((2, COMPS, NZ * WIDE, LANES), jnp.float32), pltpu.SemaphoreType.DMA((2, COMPS))],
        held=False,
    )
    def across(value, i_bits, j_bits):
        pairs = [(i * gy + j, (i ^ i_bits) * gy + (j ^ j_bits)) for i in range(gx) for j in range(gy)]
        return lax.ppermute(value, ("gx", "gy"), pairs)

    energy = sum([across(energy, 4 * k, 0) for k in range(1, gx // 4)], energy)
    energy = energy + near(energy) + across(energy, 0, 1) + across(energy, 1, 1)
    energy = energy + across(energy, 0, 2)
    parts = [energy, across(energy, 2, 3)]
    placed_first = [pltpu.with_memory_space_constraint(value, pltpu.HBM) for value in (new_q, new_p)]
    (energy,) = run(functools.partial(total_kernel, volume), [f32(1, 2)], parts, after=placed_first)
    return (new_q.reshape(field.shape), new_p.reshape(field.shape), energy)


def solution(mesh):
    placed = (
        P("rep", None, None, "gx", "gy"),
        P("rep", None, None, "gx", "gy"),
        P("rep"),
        P("rep"),
        P(),
    )
    return jax.shard_map(
        local,
        mesh=mesh,
        in_specs=placed,
        out_specs=(
            P("rep", None, None, "gx", "gy"),
            P("rep", None, None, "gx", "gy"),
            P("rep", None),
        ),
        check_vma=False,
    )
```

```python
import functools

import jax
import jax.numpy as jnp
from jax import lax
from jax.experimental import pallas as pl
from jax.experimental.pallas import tpu as pltpu
from jax.sharding import PartitionSpec as P

LEAPS = 4
STEP = 0.05
COMPS = 4
NZ = 64
OCT = NZ // 8
WIDE = 4
LANES = 128
SITES = COMPS * NZ


def f32(*shape):
    return jax.ShapeDtypeStruct(shape, jnp.float32)


def lanes():
    return lax.broadcasted_iota(jnp.int32, (8, LANES), 1)


def rows():
    return lax.broadcasted_iota(jnp.int32, (8, LANES), 0)


def packed(load):
    octet = lanes() // 16
    out = None
    for o in range(OCT):
        moved = pltpu.roll(load(o), (16 * o + 8) % LANES, 1)
        out = moved if out is None else jnp.where(octet == o, moved, out)
    return out


def layer_of(main, edge=None):
    return (lambda c, o: main[c, 8 * o : 8 * o + 8, :], None if edge is None else (lambda c: edge[c]))


def joint(ref):
    return (lambda c, o: ref[c, 8 * o : 8 * o + 8, :], lambda c: ref[c, NZ : NZ + 8, :])


def store_main(q, p):
    def put(c, o, new_p, new_q):
        if p is not None:
            p[c, 8 * o : 8 * o + 8, :] = new_p
        if q is not None:
            q[c, 8 * o : 8 * o + 8, :] = new_q

    return put


def store_edge(q, p):
    def put(c, new_p, new_q):
        p[c, NZ : NZ + 8, :] = new_p
        q[c, NZ : NZ + 8, :] = new_q

    return put


def settings(ref):
    row = lax.broadcasted_iota(jnp.int32, (LANES, LANES), 0)
    lane = lax.broadcasted_iota(jnp.int32, (LANES, LANES), 1)
    mix = jnp.where(jnp.abs(row - lane) == 1, 1.0, 0.0).astype(jnp.bfloat16)
    return (ref[0], ref[1], jnp.concatenate([mix, mix], axis=0))


def main_eval(down, here, up, mom, put, par, dt, energy):
    kap, qua, mix = par
    lane, row = (lanes(), rows())
    zero_lane, last_lane = (lane == 0, lane == LANES - 1)
    first_row, last_row = (row == 0, row == 7)
    nsums = {}
    for c in range(COMPS):
        cells = [here[0](c, o) for o in range(OCT)]
        edge = here[1](c)
        whole = jnp.concatenate(cells, axis=0)
        high = whole.astype(jnp.bfloat16)
        low = (whole - high.astype(jnp.float32)).astype(jnp.bfloat16)
        beside = jnp.dot(jnp.concatenate([high, low], axis=1), mix, preferred_element_type=jnp.float32)
        left = [pltpu.roll(edge, (121 - 16 * o) % LANES, 1) for o in range(OCT)]
        right = [pltpu.roll(edge, (119 - 16 * o) % LANES, 1) for o in range(OCT)]
        above = [pltpu.roll(q, 7, 0) for q in cells]
        below = [pltpu.roll(q, 1, 0) for q in cells]
        for o in range(OCT):
            z_up = jnp.where(last_row, above[(o + 1) % OCT], above[o])
            z_down = jnp.where(first_row, below[o - 1], below[o])
            ghost = jnp.where(zero_lane, left[o], jnp.where(last_lane, right[o], 0.0))
            y_sum = beside[8 * o : 8 * o + 8] + ghost
            nsums[c, o] = (down[0](c, o) + up[0](c, o)) + y_sum + (z_up + z_down)
    waiting = []
    for o in range(OCT):
        cells = [here[0](c, o) for c in range(COMPS)]
        moms = [mom[0](c, o) for c in range(COMPS)]
        square = cells[0] * cells[0]
        for c in range(1, COMPS):
            square = square + cells[c] * cells[c]
        coef = (2.0 - 4.0 * qua) + (4.0 * qua) * square
        dots = None
        results = []
        for c in range(COMPS):
            q, p, nsum = (cells[c], moms[c], nsums[c, o])
            new = p + dt * ((2.0 * kap) * nsum - coef * q)
            results.append((new, q + STEP * new))
            if energy is not None:
                dots = q * nsum if dots is None else dots + q * nsum
                kin = new if energy[1] else p
                energy[0] = energy[0] + 0.5 * (kin * kin)
        if energy is not None:
            energy[0] = energy[0] + (square - kap * dots + qua * ((square - 1.0) * (square - 1.0)))
        waiting.append((o, results))
        while len(waiting) > (2 if o < OCT - 1 else 0):
            at, ready = waiting.pop(0)
            for c in range(COMPS):
                put(c, at, *ready[c])


def edge_eval(jobs, par, dt):
    kap, qua, _ = par
    lane, row = (lanes(), rows())
    slot = lane % 16
    first_row, last_row = (row == 0, row == 7)
    results = []
    for down, here, up, mom, _ in jobs:
        cells = [here[1](c) for c in range(COMPS)]
        square = cells[0] * cells[0]
        for c in range(1, COMPS):
            square = square + cells[c] * cells[c]
        coef = (2.0 - 4.0 * qua) + (4.0 * qua) * square
        for c in range(COMPS):
            q = cells[c]
            own = packed(lambda o: here[0](c, o))
            right = pltpu.roll(jnp.where(slot == 8, own, q), LANES - 1, 1)
            left = pltpu.roll(jnp.where(slot == 7, own, q), 1, 1)
            above = pltpu.roll(q, 7, 0)
            below = pltpu.roll(q, 1, 0)
            z_up = jnp.where(last_row, pltpu.roll(above, LANES - 16, 1), above)
            z_down = jnp.where(first_row, pltpu.roll(below, 16, 1), below)
            nsum = (down[1](c) + up[1](c)) + (left + right) + (z_up + z_down)
            new = mom[1](c) + dt * ((2.0 * kap) * nsum - coef * q)
            results.append((new, q + STEP * new))

    def store():
        for job, (*_, put) in enumerate(jobs):
            for c in range(COMPS):
                put(c, *results[job * COMPS + c])

    return store


def ingest_kernel(flags, field, momenta, *refs):
    mains, messages, (held, sems) = ((refs[:4], refs[4:8]), refs[8:10], refs[10:])
    copies = {
        (k, c): pltpu.make_async_copy(src.at[c], held.at[k, c], sems.at[k, c])
        for c in range(COMPS)
        for k, src in enumerate((field, momenta))
    }
    for copy in copies.values():
        copy.start()
    low = lanes() % 16 < 8
    odd = flags[1] == 1
    mirrored = jnp.broadcast_to(flags[0, :1, :], (NZ, LANES)) == 1
    for c in range(COMPS):
        copies[0, c].wait()
        copies[1, c].wait()
        lines = [[held[k, c, pl.ds(x, NZ, stride=WIDE), :] for x in range(WIDE)] for k in range(2)]
        for u in range(WIDE):
            packs = []
            for k in range(2):
                value = jnp.where(mirrored, lines[k][WIDE - 1 - u], lines[k][u])
                mains[k][u][c] = value
                packs.append(packed(lambda o: value[8 * o : 8 * o + 8, :]))
            right = jnp.where(low, packs[0], pltpu.roll(packs[1], 8, 1))
            left = jnp.where(low, pltpu.roll(packs[0], LANES - 8, 1), packs[1])
            messages[0][u, c] = jnp.where(odd, left, right)
            messages[1][u, c] = jnp.where(odd, right, left)


def ghost_kernel(flags, first, second, m1, k0, qg, pg, near, far):
    low = lanes() % 16 < 8
    odd = flags[1] == 1
    for u in range(WIDE):
        for c in range(COMPS):
            left = jnp.where(odd, first[u, c], second[u, c])
            right = jnp.where(odd, second[u, c], first[u, c])
            q = jnp.where(low, left, pltpu.roll(right, 8, 1))
            p = jnp.where(low, pltpu.roll(left, LANES - 8, 1), right)
            qg[u, c] = q
            pg[u, c] = p
            if u == WIDE - 1:
                near[c] = q
    write_main(far, 0, lambda c, o: m1[c, 8 * o : 8 * o + 8, :])
    write_main(far, SITES, lambda c, o: k0[c, 8 * o : 8 * o + 8, :])
    write_edge(far, 2 * SITES, lambda c: qg[0, c])
    write_edge(far, 2 * SITES + 16, lambda c: qg[1, c])
    write_edge(far, 2 * SITES + 32, lambda c: pg[0, c])


def fresh():
    return jnp.zeros((8, LANES), jnp.float32)


def step(around, moms, outs, par, dt, energy=None, edges=True):
    spans = [around[i : i + 3] for i in range(len(moms))]
    store = None
    if edges:
        jobs = [(*span, mom, store_edge(*out)) for span, mom, out in zip(spans, moms, outs)]
        store = edge_eval(jobs, par, dt)
    for span, mom, out in zip(spans, moms, outs):
        main_eval(*span, mom, store_main(*out), par, dt, energy)
    if edges:
        store()


def inside(ref, main, edge):
    def ghosts(c):
        value = ref[edge + 8 * (c % 2) : edge + 8 * (c % 2) + 8, :]
        return value if c < 2 else pltpu.roll(value, LANES - 8, 1)

    return (lambda c, o: ref[main + NZ * c + 8 * o : main + NZ * c + 8 * o + 8, :], ghosts)


def inside_four(ref, main, edge):
    ghosts = lambda c: pltpu.roll(ref[edge : edge + 8, :], (6 - 4 * c) % LANES, 1)
    return (inside(ref, main, edge)[0], ghosts)


def write_four(ref, edge, load):
    part = lanes() % 16 // 4
    out = pltpu.roll(load(0), LANES - 6, 1)
    for c in range(1, COMPS):
        out = jnp.where(part == c, pltpu.roll(load(c), (4 * c - 6) % LANES, 1), out)
    ref[edge : edge + 8, :] = out


def write_main(ref, main, load):
    for c in range(COMPS):
        for o in range(OCT):
            ref[main + NZ * c + 8 * o : main + NZ * c + 8 * o + 8, :] = load(c, o)


def write_edge(ref, edge, load):
    slot = lanes() % 16
    for c in range(2):
        both = jnp.where((slot >= 4) & (slot < 12), load(c), pltpu.roll(load(c + 2), 8, 1))
        ref[edge + 8 * c : edge + 8 * c + 8, :] = both


def inner_start(
    par, far, m0, m1, m2, m3, k0, k1, k2, k3, qg, pg, near, near_g, z, zp, q1, p1, q2, p2, q3, p3, energy, msg, msg_near
):
    par = settings(par)
    around = [layer_of(main, qg.at[u]) for u, main in enumerate((m0, m1, m2, m3))] + [layer_of(near, near_g)]
    total = [fresh(), False]
    held = [layer_of(mom, pg.at[u + 1]) for u, mom in enumerate((k1, k2, k3))]
    step(around, held, [(q1, p1), (q2, p2), (q3, p3)], par, 0.5 * STEP, total)
    write_main(msg, 0, joint(q1)[0])
    write_four(msg, SITES, joint(q1)[1])
    write_main(msg_near, 0, joint(q3)[0])
    write_edge(msg_near, SITES, joint(q3)[1])
    store = store_main(z, zp)
    main_eval(layer_of(far), around[0], around[1], layer_of(k0), store, par, 0.5 * STEP, total)
    energy[...] = total[0]


def outer_first(par, beyond, far, m0, qg, pg, z, zp, q1, p1, q2, zg, n1, r1, hq, hp, nz, nzp, zpg):
    par = settings(par)
    outer, halo = (inside(beyond, 0, 2 * SITES + 16), inside(beyond, 0, 2 * SITES))
    halo = (layer_of(far)[0], halo[1])
    here = layer_of(m0, qg.at[0])

    def put(c, new_p, new_q):
        zpg[c] = new_p
        zg[c] = new_q

    edge_eval([(halo, here, (None, lambda c: qg[1, c]), (None, lambda c: pg[0, c]), put)], par, 0.5 * STEP)()
    step([outer, halo, here], [inside(beyond, SITES, 2 * SITES + 32)], [(hq, hp)], par, 0.5 * STEP)
    step([layer_of(z, zg), joint(q1), joint(q2)], [joint(p1)], [(n1, r1)], par, STEP)
    step([joint(hq), layer_of(z, zg), joint(q1)], [layer_of(zp, zpg)], [(nz, nzp)], par, STEP)


def inner_second(par, z, q1, p1, q2, p2, q3, p3, near, n1, r1, n2, r2, n3, r3, msg, msg_near):
    around = [joint(z), joint(q1), joint(q2), joint(q3), inside_four(near, 0, SITES)]
    moms = [joint(p1), joint(p2), joint(p3)]
    step(around, moms, [(n1, r1), (n2, r2), (n3, r3)], settings(par), STEP)
    write_main(msg, 0, joint(q1)[0])
    write_four(msg, SITES, joint(q1)[1])
    write_main(msg, SITES + 8, joint(n1)[0])
    write_main(msg_near, 0, joint(n3)[0])
    write_four(msg_near, SITES, joint(n3)[1])


def outer_kernel(par, beyond, hq, hp, zold, zold_g, z, zp, old1, q1, p1, q2, nhq, nhp, nz, nzp, n1, r1):
    par = settings(par)
    step([inside_four(beyond, 0, SITES), joint(hq), layer_of(zold, zold_g)], [joint(hp)], [(nhq, nhp)], par, STEP)
    step([joint(nhq), joint(z), joint(old1)], [joint(zp)], [(nz, nzp)], par, STEP)
    step([joint(nz), joint(q1), joint(q2)], [joint(p1)], [(n1, r1)], par, STEP)


def inner_kernel(par, q1, q2, p2, q3, p3, near, n2, r2, n3, r3, msg):
    around = [joint(q1), joint(q2), joint(q3), inside(near, 0, SITES)]
    step(around, [joint(p2), joint(p3)], [(n2, r2), (n3, r3)], settings(par), STEP)
    write_main(msg, 0, joint(n3)[0])
    write_four(msg, SITES, joint(n3)[1])


def inner_third(par, q1, q2, p2, q3, p3, near, n2, r2, n3, r3, msg, whole):
    around = [joint(q1), joint(q2), joint(q3), inside_four(near, 0, SITES)]
    step(around, [joint(p2), joint(p3)], [(n2, r2), (n3, r3)], settings(par), STEP)
    write_main(msg, 0, joint(n3)[0])
    for u, ref in enumerate((n2, n3)):
        for c in range(COMPS):
            whole[u, c] = ref[c, :NZ, :]


def inner_final(par, q1, q2, p2, q3, p3, near, r2, r3, energy):
    around = [joint(q1), joint(q2), joint(q3), inside(near, 0, 0)]
    total = [fresh(), True]
    outs = [(None, r2), (None, r3)]
    step(around, [joint(p2), joint(p3)], outs, settings(par), 0.5 * STEP, total, False)
    energy[...] = total[0]


def outer_last(
    par, beyond, hq, hp, zold, z, zp, old1, q1, p1, q2, r2, r3, start, more,
    whole, energy, nhq, nhp, nz, nzp, last,
):
    par = settings(par)
    step([inside_four(beyond, 0, SITES), joint(hq), joint(zold)], [joint(hp)], [(nhq, nhp)], par, STEP)
    step([joint(nhq), joint(z), joint(old1)], [joint(zp)], [(nz, nzp)], par, STEP)
    store = store_main(last, None)
    outer = inside(beyond, SITES + 8, 0)
    main_eval(outer, joint(nhq), joint(z), joint(nhp), store, par, STEP, None)
    total = [more[...], True]
    store = store_main(None, whole.at[2])
    main_eval(layer_of(last), joint(nz), joint(q1), joint(nzp), store, par, 0.5 * STEP, total)
    store = store_main(None, whole.at[3])
    main_eval(joint(nz), joint(q1), joint(q2), joint(p1), store, par, 0.5 * STEP, total)
    before = jnp.sum(start[...], axis=0, keepdims=True)
    after = jnp.sum(total[0], axis=0, keepdims=True)
    row = rows()
    energy[...] = jnp.where(row == 0, before, jnp.where(row == 1, after, 0.0))
    for c in range(COMPS):
        whole[0, c] = nz[c, :NZ, :]
        whole[1, c] = q1[c, :NZ, :]
        whole[4, c] = r2[c]
        whole[5, c] = r3[c]


def pack_kernel(late, out):
    out[...] = late[...]


def pick_kernel(acceptance, flags, choice):
    position = flags[2]
    partner = position
    for replica in range(acceptance.shape[0]):
        partner = jnp.where(position == replica, acceptance[replica], partner)
    beside = position ^ 1
    choice[0] = flags[0]
    choice[1] = (partner == beside).astype(jnp.int32)
    choice[2] = ((partner != beside) & (partner != position)).astype(jnp.int32)


def place_kernel(choice, *refs):
    late, early, (new_q, new_p, held, sems) = (refs[:3], refs[3:6], refs[6:])
    mirrored, first, second = (jnp.broadcast_to(choice[i, :1, :], (NZ, LANES)) == 1 for i in range(3))

    def picked(sources, u, c):
        return jnp.where(first, sources[1][u, c], jnp.where(second, sources[2][u, c], sources[0][u, c]))

    copies = []
    for k, out in enumerate((new_q, new_p)):
        for c in range(COMPS):
            if k == 1:
                layers = [picked(late, u + 2, c) for u in range(WIDE)]
            else:
                layers = [picked(late, u, c) if u < 2 else picked(early, u - 2, c) for u in range(WIDE)]
            for x in range(WIDE):
                value = jnp.where(mirrored, layers[WIDE - 1 - x], layers[x])
                held[k, c, pl.ds(x, NZ, stride=WIDE), :] = value
            copies.append(pltpu.make_async_copy(held.at[k, c], out.at[c], sems.at[k, c]))
            copies[-1].start()
    for copy in copies:
        copy.wait()


def total_kernel(volume, *refs):
    *parts, out = refs
    total = sum((ref[...] for ref in parts[1:]), parts[0][...])
    start, finish = (jnp.sum(total[i : i + 1, :], axis=1, keepdims=True) for i in range(2))
    lane = lax.broadcasted_iota(jnp.int32, (1, 2), 1)
    out[...] = jnp.where(lane == 0, start, finish) * (1.0 / volume)


def run(kernel, outs, arrays, scratch=(), raw=(), after=(), held=True, scalars=()):
    vmem, hbm = (pl.BlockSpec(memory_space=pltpu.VMEM), pl.BlockSpec(memory_space=pltpu.HBM))
    given = len(scalars) + len(arrays) + len(raw)

    def body(*refs):
        kernel(*refs[:given], *refs[given + len(after) :])

    space = pltpu.VMEM if held else pltpu.HBM
    return pl.pallas_call(
        body,
        out_shape=[space(out.shape, out.dtype) for out in outs],
        in_specs=[pl.BlockSpec(memory_space=pltpu.SMEM)] * len(scalars)
        + [vmem] * len(arrays) + [hbm] * len(raw) + [pl.BlockSpec(memory_space=pl.ANY)] * len(after),
        out_specs=[vmem if held else hbm] * len(outs),
        scratch_shapes=list(scratch),
        cost_estimate=pl.CostEstimate(flops=4000, bytes_accessed=1000, transcendentals=0),
        compiler_params=pltpu.CompilerParams(vmem_limit_bytes=12 * 1024 * 1024),
    )(
        *scalars,
        *(pltpu.with_memory_space_constraint(value, pltpu.VMEM) for value in arrays),
        *(pltpu.with_memory_space_constraint(value, pltpu.HBM) for value in raw),
        *after,
    )


def pair_swap(value, axis, other):
    return lax.ppermute(value, axis, [(i, other(i)) for i in range(lax.axis_size(axis)) if other(i) is not None])


def local(field, momenta, kappa, quartic, acceptance):
    gx, gy, reps = (lax.axis_size("gx"), lax.axis_size("gy"), lax.axis_size("rep"))
    volume = NZ * WIDE * LANES * gx * gy
    core = lax.axis_index("gx") % 2
    places = [core, lax.axis_index("gy") % 2, lax.axis_index("rep")]
    flags = jnp.broadcast_to(jnp.stack(places)[:, None, None], (3, 8, LANES)).astype(jnp.int32)
    par = jnp.broadcast_to(jnp.concatenate([kappa, quartic])[:, None, None], (2, 8, LANES))
    (choice,) = run(pick_kernel, [jax.ShapeDtypeStruct((3, 8, LANES), jnp.int32)], [flags], scalars=[acceptance])

    def far(value):
        return pair_swap(value, "gx", lambda i: (i + 1) % gx if i % 2 == 1 else (i - 1) % gx)

    def near(value):
        return pair_swap(value, "gx", lambda i: i ^ 1)

    def beside(value, parity):
        return pair_swap(value, "gy", lambda i: (i + 1) % gy if i % 2 == parity else (i - 1) % gy)

    def exchanged(value):
        first = pair_swap(value, "rep", lambda i: i ^ 1 if i ^ 1 < reps else None)
        second = pair_swap(value, "rep", lambda i: ((i - 1) ^ 1) + 1 if 0 < i and ((i - 1) ^ 1) + 1 < reps else None)
        return (first, second)

    main, both = (f32(COMPS, NZ, LANES), f32(COMPS, NZ + 8, LANES))
    edges, whole, vreg = (f32(WIDE, COMPS, 8, LANES), f32(WIDE, COMPS, NZ, LANES), f32(8, LANES))
    edge, side, slim = (f32(COMPS, 8, LANES), f32(SITES + 16, LANES), f32(SITES + 8, LANES))

    m0, m1, m2, m3, k0, k1, k2, k3, to_first, to_second = run(
        ingest_kernel,
        [main] * 8 + [edges] * 2,
        [flags],
        scratch=[pltpu.VMEM((2, COMPS, NZ * WIDE, LANES), jnp.float32), pltpu.SemaphoreType.DMA((2, COMPS))],
        raw=[value.reshape(COMPS, NZ * WIDE, LANES) for value in (field, momenta)],
    )
    far0, near0 = (far(m0), near(m3))
    first, second = (beside(to_first, 0), beside(to_second, 1))
    qg, pg, near_g, to_far = run(
        ghost_kernel, [edges, edges, edge, f32(2 * SITES + 48, LANES)], [flags, first, second, m1, k0]
    )
    near_ghost, beyond0 = (near(near_g), far(to_far))
    z1, zp1, a1, b1, a2, b2, a3, b3, start, msg, to_near = run(
        inner_start,
        [main, main] + [both] * 6 + [vreg, f32(SITES + 16, LANES), side],
        [par, far0, m0, m1, m2, m3, k0, k1, k2, k3, qg, pg, near0, near_ghost],
    )
    beyond1, near1 = (far(msg), near(to_near))
    arrays = [par, a1, a2, b2, a3, b3, near1]
    c2, d2, c3, d3, to_near = run(inner_kernel, [both] * 4 + [slim], arrays, after=[choice])
    near2 = near(to_near)
    zg1, c1, d1, hq1, hp1, z2, zp2 = run(
        outer_first,
        [edge] + [both] * 6,
        [par, beyond0, far0, m0, qg, pg, z1, zp1, a1, b1, a2],
        scratch=[pltpu.VMEM((COMPS, 8, LANES), jnp.float32)],
    )
    e1, f1, e2, f2, e3, f3, msg, to_near = run(
        inner_second,
        [both] * 6 + [f32(2 * SITES + 8, LANES), slim],
        [par, z2, c1, d1, c2, d2, c3, d3, near2],
    )
    beyond2 = far(msg)
    near3 = near(to_near)
    hq2, hp2, z3, zp3, g1, h1 = run(
        outer_kernel,
        [both] * 6,
        [par, beyond1, hq1, hp1, z1, zg1, z2, zp2, c1, e1, f1, e2],
    )
    g2, h2, g3, h3, to_near, early = run(
        inner_third,
        [both] * 4 + [f32(SITES, LANES), f32(2, COMPS, NZ, LANES)],
        [par, e1, e2, f2, e3, f3, near3],
        after=[beyond1],
    )
    near4 = near(to_near)
    first_early, second_early = exchanged(early)
    r2, r3, more = run(inner_final, [main, main, vreg], [par, g1, g2, h2, g3, h3, near4])
    late, energy = run(
        outer_last,
        [f32(6, COMPS, NZ, LANES), vreg],
        [par, beyond2, hq2, hp2, z2, z3, zp3, e1, g1, h1, g2, r2, r3, start, more],
        scratch=[pltpu.VMEM((COMPS, NZ + 8, LANES), jnp.float32)] * 4 + [pltpu.VMEM((COMPS, NZ, LANES), jnp.float32)],
    )
    (late,) = run(pack_kernel, [f32(6, COMPS, NZ, LANES)], [late], after=[first_early, second_early])
    first_late, second_late = exchanged(late)

    new_q, new_p = run(
        place_kernel,
        [f32(COMPS, NZ * WIDE, LANES)] * 2,
        [choice, late, first_late, second_late, early, first_early, second_early],
        scratch=[pltpu.VMEM((2, COMPS, NZ * WIDE, LANES), jnp.float32), pltpu.SemaphoreType.DMA((2, COMPS))],
        held=False,
    )
    def across(value, i_bits, j_bits):
        pairs = [(i * gy + j, (i ^ i_bits) * gy + (j ^ j_bits)) for i in range(gx) for j in range(gy)]
        return lax.ppermute(value, ("gx", "gy"), pairs)

    energy = sum([across(energy, 4 * k, 0) for k in range(1, gx // 4)], energy)
    energy = energy + near(energy) + across(energy, 0, 1) + across(energy, 1, 1)
    energy = energy + across(energy, 0, 2)
    parts = [energy, across(energy, 2, 3)]
    placed_first = [pltpu.with_memory_space_constraint(value, pltpu.HBM) for value in (new_q, new_p)]
    (energy,) = run(functools.partial(total_kernel, volume), [f32(1, 2)], parts, after=placed_first)
    return (new_q.reshape(field.shape), new_p.reshape(field.shape), energy)


def solution(mesh):
    placed = (
        P("rep", None, None, "gx", "gy"),
        P("rep", None, None, "gx", "gy"),
        P("rep"),
        P("rep"),
        P(),
    )
    return jax.shard_map(
        local,
        mesh=mesh,
        in_specs=placed,
        out_specs=(
            P("rep", None, None, "gx", "gy"),
            P("rep", None, None, "gx", "gy"),
            P("rep", None),
        ),
        check_vma=False,
    )
```
